256 devices in a mesh: seq: 32 (over x, z), head: 8 (over y, core).
Axes of the slice: x: 4, y: 4, z: 8, core: 2. Of those that a mesh axis runs over, the one named last changes fastest.
Arguments:
- queries: bfloat16 [4096, 4096], P('seq', 'head'), may hold values from -6 to 6
- key_vecs: bfloat16 [4096, 3, 4096], P('seq', None, 'head'), as said below
- values: bfloat16 [4096, 3, 4096], P('seq', None, 'head'), may hold values from -6 to 6
- out_gate: bfloat16 [4096, 4096], P('seq', 'head'), may hold values from -6 to 6
- beta_rates: float32 [3, 32, 4096], P(None, 'head', 'seq'), may hold values from 0 to 2
- log_decay: float32 [32, 4096], P('head', 'seq')
- norm_gain: float32 [128], replicated, may hold values from 0.1 to 1.9
- w_out: bfloat16 [4096, 4096], P('head'), may hold values from -0.09375 to 0.09375
Outputs:
- layer_out: bfloat16 [4096, 4096], P(('seq', 'head'))
The draws below stay inside these ranges and needn't reach their ends.
Inputs may be any that keep to these rules, and one draw needn't show every extreme that they name: `key_vecs`: each aligned block of 128 entries is one key.
All inputs are finite; a program needn't handle non-finite values.
Results may differ from the reference program's by a relative error of at most 0.0059.
Values sent between devices are 32-bit elements; how exact they have to be, the bound alone decides.
A program may use at most 64 MiB of HBM per device.

```python
import jax
import jax.numpy as jnp
from jax import lax

D = 4096
HEAD_TOTAL = 32
DK = 128
STEPS = 3
TOKEN_TOTAL = 4096


def slow_heads(base_key, slow_share):
    return jax.random.randint(base_key, (HEAD_TOTAL,), 0, 16) < slow_share


def draw_key_vecs(key, part):
    key = jax.random.fold_in(key, 3)
    first_key, second_key = jax.random.split(key, 2)
    entries = jax.random.normal(first_key, (TOKEN_TOTAL, STEPS, HEAD_TOTAL * DK), jnp.float32)
    row_scale = jnp.exp(jax.random.uniform(second_key, (TOKEN_TOTAL, STEPS, HEAD_TOTAL), jnp.float32, 0.0, jnp.log(10.0)))
    return (entries * jnp.repeat(row_scale, DK, axis=-1)).astype(jnp.bfloat16)


def draw_beta_rates(key, part):
    slow_mask = slow_heads(key, 8)
    key = jax.random.fold_in(key, 5)
    first_key, second_key = jax.random.split(key, 2)
    fast_rates = jax.random.uniform(first_key, (STEPS, HEAD_TOTAL, TOKEN_TOTAL), jnp.float32, 0.1, 1.9)
    slow_gap = jnp.exp(jax.random.uniform(second_key, (STEPS, HEAD_TOTAL, TOKEN_TOTAL), jnp.float32, jnp.log(0.5), jnp.log(2.0))) * 8.0 / TOKEN_TOTAL
    return jnp.where(slow_mask[None, :, None], 2.0 - slow_gap, fast_rates).astype(jnp.float32)


def draw_log_decay(key, part):
    slow_mask = slow_heads(key, 8)
    key = jax.random.fold_in(key, 7)
    first_key, second_key, key_third, key_fourth = jax.random.split(key, 4)
    fast_rate = jnp.exp(jax.random.uniform(first_key, (HEAD_TOTAL, TOKEN_TOTAL), jnp.float32, jnp.log(1.0 / 70.0), jnp.log(1.0 / 20.0)))
    slow_rate = jnp.exp(jax.random.uniform(second_key, (HEAD_TOTAL, TOKEN_TOTAL), jnp.float32, jnp.log(0.5), jnp.log(2.0))) * 0.05 / TOKEN_TOTAL
    every_rate = jnp.where(slow_mask[:, None], slow_rate, fast_rate)
    segment_locations = jax.random.randint(key_third, (HEAD_TOTAL, 2), 0, TOKEN_TOTAL)
    segment_retain = jax.random.uniform(key_fourth, (HEAD_TOTAL, 2), jnp.float32, 0.5, 0.8)
    token_places = jnp.arange(TOKEN_TOTAL)
    segment_list = jnp.sum(jnp.where(token_places[None, None, :] == segment_locations[:, :, None], jnp.log(segment_retain)[:, :, None], 0.0), axis=1)
    return (segment_list - every_rate).astype(jnp.float32)


def level_of(key, dims, cuts, low, top_value):
    def one(dim, shards_of):
        steps = jax.random.uniform(jax.random.fold_in(jax.random.fold_in(key, 6), dim), (shards_of,), jnp.float32, low / len(cuts), top_value / len(cuts))
        return jnp.repeat(jnp.exp(steps), dims[dim] // shards_of).reshape((-1,) + (1,) * (len(dims) - dim - 1))

    level = one(*cuts[0])
    for cut in cuts[1:]:
        level = level * one(*cut)
    return level


def bell_draw(own_key, extent, spread, most, pieces=(), kind=jnp.bfloat16):
    drawn = spread * jax.random.normal(own_key, extent, jnp.float32)
    if pieces:
        drawn = drawn * level_of(own_key, extent, pieces, -0.22, 0.18)
    return jnp.clip(drawn, -most, most).astype(kind)


def setup_inputs(seed: int = 0) -> dict:
    arg_keys = jax.random.split(jax.random.key(seed), 9)
    queries = bell_draw(arg_keys[0], (TOKEN_TOTAL, HEAD_TOTAL * DK), 1.0, 6.0, ((0, 32), (1, 8)))
    key_vecs = draw_key_vecs(jax.random.fold_in(arg_keys[8], 71), 0)
    values = bell_draw(arg_keys[2], (TOKEN_TOTAL, STEPS, HEAD_TOTAL * DK), 1.0, 6.0, ((0, 32), (2, 8)))
    out_gate = bell_draw(arg_keys[3], (TOKEN_TOTAL, HEAD_TOTAL * DK), 1.0, 6.0, ((0, 32), (1, 8)))
    beta_rates = draw_beta_rates(jax.random.fold_in(arg_keys[8], 71), 0)
    log_decay = draw_log_decay(jax.random.fold_in(arg_keys[8], 71), 0)
    norm_gain = jnp.clip(1.0 + 0.18 * jax.random.normal(arg_keys[6], (DK,), jnp.float32), 0.1, 1.9)
    w_out = bell_draw(arg_keys[7], (HEAD_TOTAL * DK, D), (HEAD_TOTAL * DK) ** -0.5, 0.09375, ((0, 8),))
    return {"queries": queries, "key_vecs": key_vecs, "values": values, "out_gate": out_gate, "beta_rates": beta_rates, "log_decay": log_decay, "norm_gain": norm_gain, "w_out": w_out}


def reference(queries, key_vecs, values, out_gate, beta_rates, log_decay, norm_gain, w_out):
    exact_precision_mode = lax.Precision.HIGHEST
    query_rows = queries.astype(jnp.float32).reshape(TOKEN_TOTAL, HEAD_TOTAL, DK)
    raw_keys = key_vecs.astype(jnp.float32).reshape(TOKEN_TOTAL, STEPS, HEAD_TOTAL, DK)
    unit_keys = raw_keys / jnp.sqrt(lax.optimization_barrier(jnp.sum(raw_keys * raw_keys, -1, keepdims=True)) + 1e-06)
    value_rows = values.astype(jnp.float32).reshape(TOKEN_TOTAL, STEPS, HEAD_TOTAL, DK)
    strength = jnp.transpose(beta_rates, (2, 0, 1))
    decay_rate = jnp.exp(log_decay).T

    def advance(state_matrix, token_item):
        current_query, keys_now, values_now, strength_now, decay_now = token_item
        state_matrix = decay_now[:, None, None] * state_matrix
        for inner_step in range(STEPS):
            reflect_vector = keys_now[inner_step]
            retrieved_output = jnp.einsum('su,suy->sy', reflect_vector, state_matrix, precision=exact_precision_mode)
            state_matrix = state_matrix + strength_now[inner_step][:, None, None] * reflect_vector[:, :, None] * (values_now[inner_step] - retrieved_output)[:, None, :]
        return (state_matrix, jnp.einsum('su,suy->sy', current_query, state_matrix, precision=exact_precision_mode))
    zero_memory = jnp.zeros((HEAD_TOTAL, DK, DK), jnp.float32)
    final_memory, head_out = lax.scan(advance, zero_memory, (query_rows, unit_keys, value_rows, strength, decay_rate))
    mean_square = lax.optimization_barrier(jnp.mean(head_out * head_out, -1, keepdims=True))
    normed = head_out / jnp.sqrt(mean_square + 1e-05) * norm_gain
    gate_rows = out_gate.astype(jnp.float32).reshape(TOKEN_TOTAL, HEAD_TOTAL, DK)
    gated = (normed * jax.nn.silu(gate_rows)).reshape(TOKEN_TOTAL, HEAD_TOTAL * DK).astype(jnp.bfloat16)
    return jnp.dot(gated, w_out, preferred_element_type=jnp.float32).astype(jnp.bfloat16)
```

```python
import functools

import jax
import jax.numpy as jnp
from jax import lax
from jax.experimental import pallas as pl
from jax.experimental.pallas import tpu as pltpu
from jax.sharding import PartitionSpec as P

F32 = jnp.float32
BF16 = jnp.bfloat16
EXACT = lax.Precision.HIGHEST
W = 128
STEPS = 3
MICRO = STEPS * W
HEADS = 4
BASE = 32
LINE = 8
ROWS = 4
RING = 4
CHUNKS = 4
MESH = pl.DeviceIdType.MESH


def iota(shape, dim):
    return lax.broadcasted_iota(jnp.int32, shape, dim)


def split(a):
    hi = a.astype(BF16)
    return hi, (a - hi.astype(F32)).astype(BF16)


def lhs_of(a):
    return jnp.concatenate(split(a), axis=1)


def rhs_of(b):
    pair = jnp.concatenate(split(b), axis=1)
    return jnp.concatenate([pair, pair], axis=0)


def mm(left, right):
    out = jnp.dot(left, right, preferred_element_type=F32)
    half = out.shape[1] // 2
    return out[:, :half] + out[:, half:]


def nt(a, b, precision=None):
    return lax.dot_general(
        a, b, (((1,), (1,)), ((), ())), preferred_element_type=F32, precision=precision
    )


def local_maps(k_ref, v_ref, beta_ref, decay_ref, tf_ref, x_ref, emit):
    step_i, token_i = iota((MICRO, W), 0), iota((MICRO, W), 1)
    upto = (STEPS * token_i <= step_i).astype(F32)
    decay = jnp.maximum(decay_ref[...], -110.0)
    g_col = nt(upto, decay, EXACT)
    g_row = nt(decay, upto, EXACT)
    b_col = sum(
        nt((STEPS * token_i + j == step_i).astype(F32), beta_ref[j], EXACT) for j in range(STEPS)
    )
    row_i, col_i = iota((W, W), 0), iota((W, W), 1)
    strict = row_i > col_i
    eye = (row_i == col_i).astype(F32)
    ones = jnp.ones((8, 2 * W), BF16)
    lane_block = iota((BASE, W), 1) // BASE
    r_cols, r_rows, systems, packed = [], [], [], []
    for h in range(HEADS):
        keys = k_ref[:, h * W : (h + 1) * W]
        wide = keys.astype(F32)
        squares = wide * wide
        r_c = 1.0 / jnp.sqrt(jnp.sum(squares, axis=1, keepdims=True) + 1e-6)
        r_r = 1.0 / jnp.sqrt(nt(ones, lhs_of(squares))[0:1] + 1e-6)
        r_cols.append(r_c)
        r_rows.append(r_r)
        scale = b_col[:, h : h + 1] * r_c
        blocks = {}
        for i in range(3):
            for j in range(i + 1):
                si, sj = slice(i * W, (i + 1) * W), slice(j * W, (j + 1) * W)
                gap = g_col[si, h : h + 1] - g_row[h : h + 1, sj]
                if i == j:
                    gap = jnp.where(strict, gap, 0.0)
                a = nt(keys[si], keys[sj]) * (scale[si] * r_r[:, sj]) * jnp.exp(gap)
                if i == j:
                    a = jnp.where(strict, a, 0.0)
                    packed.append(
                        sum(
                            jnp.where(lane_block == b, a[b * BASE : (b + 1) * BASE], 0.0)
                            for b in range(W // BASE)
                        )
                    )
                blocks[i, j] = a
        systems.append(blocks)
    count = len(packed)
    packed = lhs_of(jnp.concatenate(packed, axis=0))
    block_start = (col_i // BASE) * BASE
    small = [
        (iota((count, 8, W), 1) + 8 * s == iota((count, 8, W), 2) % BASE).astype(F32)
        for s in range(BASE // 8)
    ]
    for j in range(BASE - 1):
        pick = (row_i == block_start + j).astype(BF16)
        factor = jnp.dot(
            packed, jnp.concatenate([pick, pick], axis=0), preferred_element_type=F32
        ).reshape(count, BASE, W)
        first = j // 8
        row = small[first][:, j % 8 : j % 8 + 1, :]
        for s in range(first, BASE // 8):
            small[s] = small[s] - factor[:, 8 * s : 8 * s + 8, :] * row
    same32 = (row_i // 32) == (col_i // 32)
    same64 = (row_i // 64) == (col_i // 64)
    low32 = same64 & jnp.logical_not(same32)
    low64 = jnp.logical_not(same64)
    for h in range(HEADS):
        wide = k_ref[:, h * W : (h + 1) * W].astype(F32)
        inverse = []
        for i in range(3):
            n = h * 3 + i
            tile = jnp.concatenate([small[s][n] for s in range(BASE // 8)], axis=0)
            inv = jnp.where(same32, jnp.concatenate([tile] * (W // BASE), axis=0), 0.0)
            for low in (low32, low64):
                step = mm(lhs_of(inv), rhs_of(jnp.where(low, systems[h][i, i], 0.0)))
                inv = inv - mm(lhs_of(step), rhs_of(inv))
            inverse.append(lhs_of(inv))
        b_c, g_c = b_col[:, h : h + 1], g_col[:, h : h + 1]
        right = jnp.concatenate(
            [
                b_c * v_ref[:, h * W : (h + 1) * W].astype(F32),
                (b_c * jnp.exp(g_c) * r_cols[h]) * wide,
            ],
            axis=1,
        )
        x1 = mm(inverse[0], rhs_of(right[:W]))
        x1r = rhs_of(x1)
        x2 = mm(inverse[1], rhs_of(right[W : 2 * W] - mm(lhs_of(systems[h][1, 0]), x1r)))
        x3 = mm(
            inverse[2],
            rhs_of(
                right[2 * W :]
                - mm(lhs_of(systems[h][2, 0]), x1r)
                - mm(lhs_of(systems[h][2, 1]), rhs_of(x2))
            ),
        )
        solved = jnp.concatenate([x1, x2, x3], axis=0)
        x_ref[h] = rhs_of(solved)
        g_end = g_col[MICRO - 1 : MICRO, h : h + 1]
        tail = jnp.concatenate(split((r_cols[h] * jnp.exp(g_end - g_c)) * solved), axis=1)
        out = jnp.dot(wide.T.astype(BF16), tail, preferred_element_type=F32)
        out = out[:, : 2 * W] + out[:, 2 * W :]
        tf_ref[h, 0] = jnp.exp(g_end) * eye - out[:, W:]
        tf_ref[h, 1] = out[:, :W]
        emit(h)
    return g_row, r_rows


def local_reads(q_ref, k_ref, decay_ref, x_ref, g_row, r_rows, lo_ref, lq_ref):
    decay = jnp.maximum(decay_ref[...], -110.0)
    upto = (iota((W, W), 1) <= iota((W, W), 0)).astype(F32)
    q_col = nt(upto, decay, EXACT)
    visible = iota((W, MICRO), 1) <= STEPS * iota((W, MICRO), 0) + STEPS - 1
    for h in range(HEADS):
        keys = k_ref[:, h * W : (h + 1) * W]
        query = q_ref[:, h * W : (h + 1) * W]
        gap = jnp.where(visible, q_col[:, h : h + 1] - g_row[h : h + 1, :], 0.0)
        scores = jnp.where(visible, nt(query, keys) * (r_rows[h] * jnp.exp(gap)), 0.0)
        reads = mm(lhs_of(scores), x_ref[h])
        lo_ref[h] = reads[:, :W]
        lq_ref[h] = lhs_of(jnp.exp(q_col[:, h : h + 1]) * query.astype(F32) - reads[:, W:])


def compose(lefts, right):
    out = mm(
        jnp.concatenate([lhs_of(t) for t, f in lefts], axis=0),
        rhs_of(jnp.concatenate(right, axis=1)),
    )
    return [
        (out[i * W : (i + 1) * W, :W], out[i * W : (i + 1) * W, W:] + lefts[i][1])
        for i in range(len(lefts))
    ]


def layer_kernel(
    q_ref, k_ref, v_ref, gate_ref, beta_ref, decay_ref, gain_ref, w_hbm, out_ref,
    w_ref, tf_ref, x_ref, lo_ref, lq_ref, act_ref,
    maps_ref, pre_t_ref, pre_f_ref, total_ref, far_ref, line_ref, next_ref, given_ref, start_ref,
    gated_ref, pair_out, pair_in, own_ref, relay_in, side_in,
    w_sem, map_send, map_recv, line_send, line_recv, start_send, start_recv,
    pair_send, pair_recv, ring_send, ring_recv,
):
    seq, head = lax.axis_index("seq"), lax.axis_index("head")
    x, z = seq // LINE, lax.rem(seq, LINE)
    y, core = head // 2, lax.rem(head, 2)
    line = x * LINE

    def at(s, h):
        return {"device_id": (s, h), "device_id_type": MESH}

    up = lax.rem(y + 1, RING) * 2 + core
    down = lax.rem(y + RING - 1, RING) * 2 + core
    sibling = y * 2 + 1 - core

    w_copy = pltpu.make_async_copy(w_hbm, w_ref, w_sem)
    w_copy.start()

    barrier = pltpu.get_barrier_semaphore()
    for i in range(1, LINE):
        pl.semaphore_signal(barrier, inc=1, **at(line + lax.rem(z + i, LINE), head))
    for i in range(1, ROWS):
        pl.semaphore_signal(barrier, inc=1, **at(lax.rem(x + i, ROWS) * LINE + z, head))
    for h in (up, down, sibling):
        pl.semaphore_signal(barrier, inc=1, **at(seq, h))
    pl.semaphore_wait(barrier, LINE - 1 + ROWS - 1 + 3)

    def map_copy(h):
        return pltpu.make_async_remote_copy(
            src_ref=tf_ref.at[h], dst_ref=maps_ref.at[z],
            send_sem=map_send.at[h], recv_sem=map_recv.at[z], **at(line + 2 * h, head),
        )

    def emit(h):
        @pl.when(z != 2 * h)
        def _():
            map_copy(h).start()

        @pl.when(z == 2 * h)
        def _():
            maps_ref[z] = tf_ref[h]

    g_row, r_rows = local_maps(k_ref, v_ref, beta_ref, decay_ref, tf_ref, x_ref, emit)
    local_reads(q_ref, k_ref, decay_ref, x_ref, g_row, r_rows, lo_ref, lq_ref)
    gate = gate_ref[...].astype(F32)
    act_ref[...] = (gate / (1.0 + jnp.exp(-gate))) * jnp.concatenate([gain_ref[...]] * HEADS, axis=1)

    owner = lax.rem(z, 2) == 0
    mine = z // 2

    def line_copy(src, dst, send, recv, to):
        return pltpu.make_async_remote_copy(
            src_ref=src, dst_ref=dst, send_sem=line_send.at[send], recv_sem=line_recv.at[recv],
            **at(to * LINE + z, head),
        )

    @pl.when(owner)
    def _():
        for i in range(1, LINE):
            other = lax.rem(z + i, LINE)
            pltpu.make_async_remote_copy(
                src_ref=tf_ref.at[0], dst_ref=maps_ref.at[other],
                send_sem=map_send.at[0], recv_sem=map_recv.at[other], **at(line + other, head),
            ).wait_recv()
        m = [(maps_ref[i, 0], maps_ref[i, 1]) for i in range(LINE)]
        (p1,) = compose([m[1]], m[0])
        (q23,) = compose([m[3]], m[2])
        (q45,) = compose([m[5]], m[4])
        (q67,) = compose([m[7]], m[6])
        p2, p3 = compose([m[2], q23], p1)
        q46, q47 = compose([m[6], q67], q45)
        p4, p5, p6, p7 = compose([m[4], q45, q46, q47], p3)
        total_ref[0] = p7[0]
        total_ref[1] = p7[1]
        for i, (t, f) in enumerate((m[0], p1, p2, p3, p4, p5, p6, p7)):
            pre_t_ref[i * W : (i + 1) * W] = lhs_of(t)
            pre_f_ref[i] = f

        @pl.when(x == 0)
        def _():
            line_copy(total_ref.at[1], line_ref, 0, 0, 1).start()

        @pl.when(x == 2)
        def _():
            line_copy(total_ref, far_ref, 0, 1, 3).start()

        @pl.when(x > 0)
        def _():
            line_copy(total_ref.at[1], line_ref, 0, 0, 1).wait_recv()

        @pl.when(x == 1)
        def _():
            next_ref[...] = mm(pre_t_ref[7 * W :], rhs_of(line_ref[...])) + pre_f_ref[7]
            line_copy(next_ref, line_ref, 0, 0, 3).start()
            line_copy(next_ref, line_ref, 1, 0, 2).start()

        @pl.when(x == 3)
        def _():
            line_copy(total_ref, far_ref, 0, 1, 3).wait_recv()
            next_ref[...] = mm(lhs_of(far_ref[0]), rhs_of(line_ref[...])) + far_ref[1]

        @pl.when(x == 0)
        def _():
            given_ref[0] = jnp.zeros((W, W), F32)
            for i in range(1, LINE):
                given_ref[i] = pre_f_ref[i - 1]

        @pl.when(x > 0)
        def _():
            begin = jnp.where(x == 3, next_ref[...], line_ref[...])
            after = mm(pre_t_ref[: 7 * W], rhs_of(begin))
            given_ref[0] = begin
            for i in range(1, LINE):
                given_ref[i] = after[(i - 1) * W : i * W] + pre_f_ref[i - 1]

        for i in (4, 5, 3, 6, 2, 7, 1):
            other = lax.rem(z + i, LINE)
            pltpu.make_async_remote_copy(
                src_ref=given_ref.at[other], dst_ref=start_ref.at[mine],
                send_sem=start_send.at[i], recv_sem=start_recv.at[mine], **at(line + other, head),
            ).start()
        start_ref[mine] = given_ref[z]

    for h in range(HEADS):
        @pl.when(z != 2 * h)
        def _():
            pltpu.make_async_remote_copy(
                src_ref=given_ref.at[0], dst_ref=start_ref.at[h],
                send_sem=start_send.at[0], recv_sem=start_recv.at[h], **at(line + 2 * h, head),
            ).wait_recv()

        heads_out = lo_ref[h] + mm(lq_ref[h], rhs_of(start_ref[h]))
        mean = jnp.sum(heads_out * heads_out, axis=1, keepdims=True) * (1.0 / W)
        normed = heads_out / jnp.sqrt(mean + 1e-5)
        gated_ref[:, :, h * W : (h + 1) * W] = (
            (normed * act_ref[:, h * W : (h + 1) * W]).astype(BF16).reshape(2 * RING, 16, W)
        )

    w_copy.wait()
    block = [lax.rem(y + i, RING) * 2 for i in range(RING)]
    rows = jnp.concatenate(
        [gated_ref[b + 1 - core] for b in block] + [gated_ref[b + core] for b in block], axis=0
    )
    width = w_ref.shape[1] // CHUNKS

    def pair_copy(c):
        return pltpu.make_async_remote_copy(
            src_ref=pair_out.at[c], dst_ref=pair_in.at[c],
            send_sem=pair_send.at[c], recv_sem=pair_recv.at[c], **at(seq, sibling),
        )

    order = (0, 2, 1, 3)
    for c in order:
        part = jnp.dot(rows, w_ref[:, c * width : (c + 1) * width], preferred_element_type=F32)
        pair_out[c] = part[:64].reshape(RING, 16, width)
        pair_copy(c).start()
        own_ref[c] = part[64:].reshape(RING, 16, width)

    def ring_copy(kind, c, src, dst, to):
        return pltpu.make_async_remote_copy(
            src_ref=src, dst_ref=dst, send_sem=ring_send.at[kind, c], recv_sem=ring_recv.at[kind, c],
            **at(seq, to),
        )

    def relay_copy(c):
        return ring_copy(0, c, own_ref.at[c, 2], relay_in.at[c], up if c < 2 else down)

    def up_copy(c):
        return ring_copy(1, c, own_ref.at[c, 1], side_in.at[0, c], up)

    def down_copy(c):
        return ring_copy(2, c, own_ref.at[c, 3], side_in.at[1, c], down)

    for c in order:
        pair_copy(c).wait_recv()
        own_ref[c] = own_ref[c] + pair_in[c]
        relay_copy(c).start()
        (down_copy if c < 2 else up_copy)(c).start()
    for c in order:
        relay_copy(c).wait_recv()
        if c < 2:
            own_ref[c, 1] = own_ref[c, 1] + relay_in[c]
            up_copy(c).start()
        else:
            own_ref[c, 3] = own_ref[c, 3] + relay_in[c]
            down_copy(c).start()
    for c in order:
        up_copy(c).wait_recv()
        down_copy(c).wait_recv()
        out_ref[:, c * width : (c + 1) * width] = (
            own_ref[c, 0] + side_in[0, c] + side_in[1, c]
        ).astype(BF16)

    for h in range(HEADS):
        @pl.when(z != 2 * h)
        def _():
            map_copy(h).wait_send()

    @pl.when(owner)
    def _():
        @pl.when(x == 0)
        def _():
            line_copy(total_ref.at[1], line_ref, 0, 0, 1).wait_send()

        @pl.when(x == 2)
        def _():
            line_copy(total_ref, far_ref, 0, 1, 3).wait_send()

        @pl.when(x == 1)
        def _():
            line_copy(next_ref, line_ref, 0, 0, 3).wait_send()
            line_copy(next_ref, line_ref, 1, 0, 2).wait_send()

        for i in range(1, LINE):
            other = lax.rem(z + i, LINE)
            pltpu.make_async_remote_copy(
                src_ref=given_ref.at[other], dst_ref=start_ref.at[mine],
                send_sem=start_send.at[i], recv_sem=start_recv.at[mine], **at(line + other, head),
            ).wait_send()

    for c in order:
        pair_copy(c).wait_send()
        relay_copy(c).wait_send()
        up_copy(c).wait_send()
        down_copy(c).wait_send()


def on_device(queries, key_vecs, values, out_gate, beta_rates, log_decay, norm_gain, w_out):
    inner, outer = w_out.shape
    width = outer // CHUNKS
    vmem = pl.BlockSpec(memory_space=pltpu.VMEM)
    dma = pltpu.SemaphoreType.DMA
    square = (W, W)
    return pl.pallas_call(
        layer_kernel,
        name="layer",
        out_shape=jax.ShapeDtypeStruct((16, outer), BF16),
        in_specs=[vmem] * 7 + [pl.BlockSpec(memory_space=pl.ANY)],
        out_specs=vmem,
        scratch_shapes=[
            pltpu.VMEM((inner, outer), BF16),
            pltpu.VMEM((HEADS, 2) + square, F32),
            pltpu.VMEM((HEADS, 2 * MICRO, 4 * W), BF16),
            pltpu.VMEM((HEADS,) + square, F32),
            pltpu.VMEM((HEADS, W, 2 * W), BF16),
            pltpu.VMEM((W, inner), F32),
            pltpu.VMEM((LINE, 2) + square, F32),
            pltpu.VMEM((LINE * W, 2 * W), BF16),
            pltpu.VMEM((LINE,) + square, F32),
            pltpu.VMEM((2,) + square, F32),
            pltpu.VMEM((2,) + square, F32),
            pltpu.VMEM(square, F32),
            pltpu.VMEM(square, F32),
            pltpu.VMEM((LINE,) + square, F32),
            pltpu.VMEM((HEADS,) + square, F32),
            pltpu.VMEM((2 * RING, 16, inner), BF16),
            pltpu.VMEM((CHUNKS, RING, 16, width), F32),
            pltpu.VMEM((CHUNKS, RING, 16, width), F32),
            pltpu.VMEM((CHUNKS, RING, 16, width), F32),
            pltpu.VMEM((CHUNKS, 16, width), F32),
            pltpu.VMEM((2, CHUNKS, 16, width), F32),
            dma,
            dma((HEADS,)),
            dma((LINE,)),
            dma((2,)),
            dma((2,)),
            dma((LINE,)),
            dma((HEADS,)),
            dma((CHUNKS,)),
            dma((CHUNKS,)),
            dma((3, CHUNKS)),
            dma((3, CHUNKS)),
        ],
        compiler_params=pltpu.CompilerParams(
            collective_id=0, has_side_effects=True, vmem_limit_bytes=56 * 1024 * 1024
        ),
    )(
        queries,
        key_vecs.reshape(MICRO, inner),
        values.reshape(MICRO, inner),
        out_gate,
        beta_rates,
        log_decay,
        norm_gain.reshape(1, W),
        w_out,
    )


def solution(mesh):
    placed = (
        P("seq", "head"),
        P("seq", None, "head"),
        P("seq", None, "head"),
        P("seq", "head"),
        P(None, "head", "seq"),
        P("head", "seq"),
        P(),
        P("head", None),
    )
    return jax.shard_map(
        on_device, mesh=mesh, in_specs=placed, out_specs=P(("seq", "head"), None), check_vma=False
    )
```

```python
import functools

import jax
import jax.numpy as jnp
from jax import lax
from jax.experimental import pallas as pl
from jax.experimental.pallas import tpu as pltpu
from jax.sharding import PartitionSpec as P

F32 = jnp.float32
BF16 = jnp.bfloat16
EXACT = lax.Precision.HIGHEST
W = 128
STEPS = 3
MICRO = STEPS * W
HEADS = 4
BASE = 32
LINE = 8
ROWS = 4
RING = 4
CHUNKS = 4
MESH = pl.DeviceIdType.MESH


def iota(shape, dim):
    return lax.broadcasted_iota(jnp.int32, shape, dim)


def split(a):
    hi = a.astype(BF16)
    return hi, (a - hi.astype(F32)).astype(BF16)


def lhs_of(a):
    return jnp.concatenate(split(a), axis=1)


def rhs_of(b):
    pair = jnp.concatenate(split(b), axis=1)
    return jnp.concatenate([pair, pair], axis=0)


def mm(left, right):
    out = jnp.dot(left, right, preferred_element_type=F32)
    half = out.shape[1] // 2
    return out[:, :half] + out[:, half:]


def nt(a, b, precision=None):
    return lax.dot_general(
        a, b, (((1,), (1,)), ((), ())), preferred_element_type=F32, precision=precision
    )


def local_maps(k_ref, v_ref, beta_ref, decay_ref, tf_ref, x_ref, emit):
    step_i, token_i = iota((MICRO, W), 0), iota((MICRO, W), 1)
    upto = (STEPS * token_i <= step_i).astype(F32)
    decay = jnp.maximum(decay_ref[...], -110.0)
    g_col = nt(upto, decay, EXACT)
    g_row = nt(decay, upto, EXACT)
    b_col = sum(
        nt((STEPS * token_i + j == step_i).astype(F32), beta_ref[j], EXACT) for j in range(STEPS)
    )
    row_i, col_i = iota((W, W), 0), iota((W, W), 1)
    strict = row_i > col_i
    eye = (row_i == col_i).astype(F32)
    ones = jnp.ones((8, 2 * W), BF16)
    lane_block = iota((BASE, W), 1) // BASE
    r_cols, r_rows, systems, packed = [], [], [], []
    for h in range(HEADS):
        keys = k_ref[:, h * W : (h + 1) * W]
        wide = keys.astype(F32)
        squares = wide * wide
        r_c = 1.0 / jnp.sqrt(jnp.sum(squares, axis=1, keepdims=True) + 1e-6)
        r_r = 1.0 / jnp.sqrt(nt(ones, lhs_of(squares))[0:1] + 1e-6)
        r_cols.append(r_c)
        r_rows.append(r_r)
        scale = b_col[:, h : h + 1] * r_c
        blocks = {}
        for i in range(3):
            for j in range(i + 1):
                si, sj = slice(i * W, (i + 1) * W), slice(j * W, (j + 1) * W)
                gap = g_col[si, h : h + 1] - g_row[h : h + 1, sj]
                if i == j:
                    gap = jnp.where(strict, gap, 0.0)
                a = nt(keys[si], keys[sj]) * (scale[si] * r_r[:, sj]) * jnp.exp(gap)
                if i == j:
                    a = jnp.where(strict, a, 0.0)
                    packed.append(
                        sum(
                            jnp.where(lane_block == b, a[b * BASE : (b + 1) * BASE], 0.0)
                            for b in range(W // BASE)
                        )
                    )
                blocks[i, j] = a
        systems.append(blocks)
    count = len(packed)
    packed = lhs_of(jnp.concatenate(packed, axis=0))
    block_start = (col_i // BASE) * BASE
    small = [
        (iota((count, 8, W), 1) + 8 * s == iota((count, 8, W), 2) % BASE).astype(F32)
        for s in range(BASE // 8)
    ]
    for j in range(BASE - 1):
        pick = (row_i == block_start + j).astype(BF16)
        factor = jnp.dot(
            packed, jnp.concatenate([pick, pick], axis=0), preferred_element_type=F32
        ).reshape(count, BASE, W)
        first = j // 8
        row = small[first][:, j % 8 : j % 8 + 1, :]
        for s in range(first, BASE // 8):
            small[s] = small[s] - factor[:, 8 * s : 8 * s + 8, :] * row
    same32 = (row_i // 32) == (col_i // 32)
    same64 = (row_i // 64) == (col_i // 64)
    low32 = same64 & jnp.logical_not(same32)
    low64 = jnp.logical_not(same64)
    for h in range(HEADS):
        wide = k_ref[:, h * W : (h + 1) * W].astype(F32)
        inverse = []
        for i in range(3):
            n = h * 3 + i
            tile = jnp.concatenate([small[s][n] for s in range(BASE // 8)], axis=0)
            inv = jnp.where(same32, jnp.concatenate([tile] * (W // BASE), axis=0), 0.0)
            for low in (low32, low64):
                step = mm(lhs_of(inv), rhs_of(jnp.where(low, systems[h][i, i], 0.0)))
                inv = inv - mm(lhs_of(step), rhs_of(inv))
            inverse.append(lhs_of(inv))
        b_c, g_c = b_col[:, h : h + 1], g_col[:, h : h + 1]
        right = jnp.concatenate(
            [
                b_c * v_ref[:, h * W : (h + 1) * W].astype(F32),
                (b_c * jnp.exp(g_c) * r_cols[h]) * wide,
            ],
            axis=1,
        )
        x1 = mm(inverse[0], rhs_of(right[:W]))
        x1r = rhs_of(x1)
        x2 = mm(inverse[1], rhs_of(right[W : 2 * W] - mm(lhs_of(systems[h][1, 0]), x1r)))
        x3 = mm(
            inverse[2],
            rhs_of(
                right[2 * W :]
                - mm(lhs_of(systems[h][2, 0]), x1r)
                - mm(lhs_of(systems[h][2, 1]), rhs_of(x2))
            ),
        )
        solved = jnp.concatenate([x1, x2, x3], axis=0)
        x_ref[h] = rhs_of(solved)
        g_end = g_col[MICRO - 1 : MICRO, h : h + 1]
        tail = jnp.concatenate(split((r_cols[h] * jnp.exp(g_end - g_c)) * solved), axis=1)
        out = jnp.dot(wide.T.astype(BF16), tail, preferred_element_type=F32)
        out = out[:, : 2 * W] + out[:, 2 * W :]
        tf_ref[h, 0] = jnp.exp(g_end) * eye - out[:, W:]
        tf_ref[h, 1] = out[:, :W]
        emit(h)
    return g_row, r_rows


def local_reads(q_ref, k_ref, decay_ref, x_ref, g_row, r_rows, lo_ref, lq_ref):
    decay = jnp.maximum(decay_ref[...], -110.0)
    upto = (iota((W, W), 1) <= iota((W, W), 0)).astype(F32)
    q_col = nt(upto, decay, EXACT)
    visible = iota((W, MICRO), 1) <= STEPS * iota((W, MICRO), 0) + STEPS - 1
    for h in range(HEADS):
        keys = k_ref[:, h * W : (h + 1) * W]
        query = q_ref[:, h * W : (h + 1) * W]
        gap = jnp.where(visible, q_col[:, h : h + 1] - g_row[h : h + 1, :], 0.0)
        scores = jnp.where(visible, nt(query, keys) * (r_rows[h] * jnp.exp(gap)), 0.0)
        reads = mm(lhs_of(scores), x_ref[h])
        lo_ref[h] = reads[:, :W]
        lq_ref[h] = lhs_of(jnp.exp(q_col[:, h : h + 1]) * query.astype(F32) - reads[:, W:])


def compose(lefts, right):
    out = mm(
        jnp.concatenate([lhs_of(t) for t, f in lefts], axis=0),
        rhs_of(jnp.concatenate(right, axis=1)),
    )
    return [
        (out[i * W : (i + 1) * W, :W], out[i * W : (i + 1) * W, W:] + lefts[i][1])
        for i in range(len(lefts))
    ]


def layer_kernel(
    q_ref, k_ref, v_ref, gate_ref, beta_ref, decay_ref, gain_ref, w_hbm, out_ref,
    w_ref, keys_ref, values_ref, tf_ref, x_ref, lo_ref, lq_ref, act_ref,
    maps_ref, pre_t_ref, pre_f_ref, total_ref, far_ref, line_ref, next_ref, given_ref, start_ref,
    gated_ref, pair_out, pair_in, own_ref, relay_in, side_in,
    w_sem, map_send, map_recv, line_send, line_recv, start_send, start_recv,
    pair_send, pair_recv, ring_send, ring_recv,
):
    seq, head = lax.axis_index("seq"), lax.axis_index("head")
    x, z = seq // LINE, lax.rem(seq, LINE)
    y, core = head // 2, lax.rem(head, 2)
    line = x * LINE
    owner = lax.rem(z, 2) == core
    mine = z // 2
    width = w_ref.shape[1] // CHUNKS
    order = (0, 2, 1, 3)
    held = {}

    def at(s, h):
        return {"device_id": (s, h), "device_id_type": MESH}

    up = lax.rem(y + 1, RING) * 2 + core
    down = lax.rem(y + RING - 1, RING) * 2 + core
    sibling = y * 2 + 1 - core

    w_copy = pltpu.make_async_copy(w_hbm, w_ref, w_sem)
    w_copy.start()

    barrier = pltpu.get_barrier_semaphore()
    for i in range(1, LINE):
        pl.semaphore_signal(barrier, inc=1, **at(line + lax.rem(z + i, LINE), head))
    for i in range(1, ROWS):
        pl.semaphore_signal(barrier, inc=1, **at(lax.rem(x + i, ROWS) * LINE + z, head))
    for h in (up, down, sibling):
        pl.semaphore_signal(barrier, inc=1, **at(seq, h))

    def map_copy(h):
        return pltpu.make_async_remote_copy(
            src_ref=tf_ref.at[h], dst_ref=maps_ref.at[z],
            send_sem=map_send.at[h], recv_sem=map_recv.at[z], **at(line + 2 * h + core, head),
        )

    def line_copy(src, dst, send, recv, to):
        return pltpu.make_async_remote_copy(
            src_ref=src, dst_ref=dst, send_sem=line_send.at[send], recv_sem=line_recv.at[recv],
            **at(to * LINE + z, head),
        )

    def start_copy(i, h):
        other = lax.rem(z + i, LINE)
        return pltpu.make_async_remote_copy(
            src_ref=given_ref.at[other], dst_ref=start_ref.at[h],
            send_sem=start_send.at[i], recv_sem=start_recv.at[h], **at(line + other, head),
        )

    def pair_copy(c):
        return pltpu.make_async_remote_copy(
            src_ref=pair_out.at[c], dst_ref=pair_in.at[c],
            send_sem=pair_send.at[c], recv_sem=pair_recv.at[c], **at(seq, sibling),
        )

    def ring_copy(kind, c, src, dst, to):
        return pltpu.make_async_remote_copy(
            src_ref=src, dst_ref=dst, send_sem=ring_send.at[kind, c], recv_sem=ring_recv.at[kind, c],
            **at(seq, to),
        )

    def relay_copy(c):
        return ring_copy(0, c, own_ref.at[c, 2], relay_in.at[c], up if c < 2 else down)

    def up_copy(c):
        return ring_copy(1, c, own_ref.at[c, 1], side_in.at[0, c], up)

    def down_copy(c):
        return ring_copy(2, c, own_ref.at[c, 3], side_in.at[1, c], down)

    def run_maps():
        to_time = (STEPS * lax.rem(iota((MICRO, MICRO), 1), W) + iota((MICRO, MICRO), 1) // W == iota((MICRO, MICRO), 0)).astype(BF16)
        for src, dst in ((k_ref, keys_ref), (v_ref, values_ref)):
            flat = src[...].reshape(MICRO, HEADS * W)
            dst[...] = jnp.dot(to_time, flat, preferred_element_type=F32).astype(BF16)

        def emit(h):
            if h == 0:
                pl.semaphore_wait(barrier, LINE - 1 + ROWS - 1 + 3)

            @pl.when(z != 2 * h + core)
            def _():
                map_copy(h).start()

            @pl.when(z == 2 * h + core)
            def _():
                maps_ref[z] = tf_ref[h]

        held["rows"] = local_maps(keys_ref, values_ref, beta_ref, decay_ref, tf_ref, x_ref, emit)

    def end_maps():
        for h in range(HEADS):
            @pl.when(z != 2 * h + core)
            def _():
                map_copy(h).wait_send()

    def run_reads():
        g_row, r_rows = held["rows"]
        local_reads(q_ref, keys_ref, decay_ref, x_ref, g_row, r_rows, lo_ref, lq_ref)
        gate = gate_ref[...].astype(F32)
        act_ref[...] = (gate / (1.0 + jnp.exp(-gate))) * jnp.concatenate(
            [gain_ref[...]] * HEADS, axis=1
        )

    def run_gather():
        @pl.when(owner)
        def _():
            for i in range(1, LINE):
                other = lax.rem(z + i, LINE)
                pltpu.make_async_remote_copy(
                    src_ref=tf_ref.at[0], dst_ref=maps_ref.at[other],
                    send_sem=map_send.at[0], recv_sem=map_recv.at[other], **at(line + other, head),
                ).wait_recv()

    def run_compose():
        @pl.when(owner)
        def _():
            m = [(maps_ref[i, 0], maps_ref[i, 1]) for i in range(LINE)]
            (p1,) = compose([m[1]], m[0])
            (q23,) = compose([m[3]], m[2])
            (q45,) = compose([m[5]], m[4])
            (q67,) = compose([m[7]], m[6])
            p2, p3 = compose([m[2], q23], p1)
            q46, q47 = compose([m[6], q67], q45)
            p4, p5, p6, p7 = compose([m[4], q45, q46, q47], p3)
            total_ref[0] = p7[0]
            total_ref[1] = p7[1]
            for i, (t, f) in enumerate((m[0], p1, p2, p3, p4, p5, p6, p7)):
                pre_t_ref[i * W : (i + 1) * W] = lhs_of(t)
                pre_f_ref[i] = f

    def run_lines():
        @pl.when(owner)
        def _():
            @pl.when(x == 0)
            def _():
                line_copy(total_ref.at[1], line_ref, 0, 0, 1).start()

            @pl.when(x == 2)
            def _():
                line_copy(total_ref, far_ref, 0, 1, 3).start()

            @pl.when(x > 0)
            def _():
                line_copy(total_ref.at[1], line_ref, 0, 0, 1).wait_recv()

            @pl.when(x == 1)
            def _():
                next_ref[...] = mm(pre_t_ref[7 * W :], rhs_of(line_ref[...])) + pre_f_ref[7]
                line_copy(next_ref, line_ref, 0, 0, 3).start()
                line_copy(next_ref, line_ref, 1, 0, 2).start()

            @pl.when(x == 3)
            def _():
                line_copy(total_ref, far_ref, 0, 1, 3).wait_recv()
                next_ref[...] = mm(lhs_of(far_ref[0]), rhs_of(line_ref[...])) + far_ref[1]

            @pl.when(x == 0)
            def _():
                given_ref[0] = jnp.zeros((W, W), F32)
                for i in range(1, LINE):
                    given_ref[i] = pre_f_ref[i - 1]

            @pl.when(x > 0)
            def _():
                begin = jnp.where(x == 3, next_ref[...], line_ref[...])
                after = mm(pre_t_ref[: 7 * W], rhs_of(begin))
                given_ref[0] = begin
                for i in range(1, LINE):
                    given_ref[i] = after[(i - 1) * W : i * W] + pre_f_ref[i - 1]

    def end_lines():
        @pl.when(owner)
        def _():
            @pl.when(x == 0)
            def _():
                line_copy(total_ref.at[1], line_ref, 0, 0, 1).wait_send()

            @pl.when(x == 2)
            def _():
                line_copy(total_ref, far_ref, 0, 1, 3).wait_send()

            @pl.when(x == 1)
            def _():
                line_copy(next_ref, line_ref, 0, 0, 3).wait_send()
                line_copy(next_ref, line_ref, 1, 0, 2).wait_send()

    def run_starts():
        @pl.when(owner)
        def _():
            for i in (4, 5, 3, 6, 2, 7, 1):
                start_copy(i, mine).start()
            start_ref[mine] = given_ref[z]

        for h in range(HEADS):
            @pl.when(z != 2 * h + core)
            def _():
                start_copy(1, h).wait_recv()

    def end_starts():
        @pl.when(owner)
        def _():
            for i in range(1, LINE):
                start_copy(i, mine).wait_send()

    def run_gated():
        for h in range(HEADS):
            heads_out = lo_ref[h] + mm(lq_ref[h], rhs_of(start_ref[h]))
            mean = jnp.sum(heads_out * heads_out, axis=1, keepdims=True) * (1.0 / W)
            normed = heads_out / jnp.sqrt(mean + 1e-5)
            gated_ref[:, :, h * W : (h + 1) * W] = (
                (normed * act_ref[:, h * W : (h + 1) * W]).astype(BF16).reshape(2 * RING, 16, W)
            )

    def run_project():
        w_copy.wait()
        block = [lax.rem(y + i, RING) * 2 for i in range(RING)]
        rows = jnp.concatenate(
            [gated_ref[b + 1 - core] for b in block] + [gated_ref[b + core] for b in block], axis=0
        )
        for c in order:
            part = jnp.dot(rows, w_ref[:, c * width : (c + 1) * width], preferred_element_type=F32)
            pair_out[c] = part[:64].reshape(RING, 16, width)
            pair_copy(c).start()
            own_ref[c] = part[64:].reshape(RING, 16, width)

    def run_pair():
        for c in order:
            pair_copy(c).wait_recv()
            own_ref[c] = own_ref[c] + pair_in[c]

    def end_pair():
        for c in order:
            pair_copy(c).wait_send()

    def run_ring():
        for c in order:
            relay_copy(c).start()
            (down_copy if c < 2 else up_copy)(c).start()
        for c in order:
            relay_copy(c).wait_recv()
            if c < 2:
                own_ref[c, 1] = own_ref[c, 1] + relay_in[c]
                up_copy(c).start()
            else:
                own_ref[c, 3] = own_ref[c, 3] + relay_in[c]
                down_copy(c).start()
        for c in order:
            up_copy(c).wait_recv()
            down_copy(c).wait_recv()
            out_ref[:, c * width : (c + 1) * width] = (
                own_ref[c, 0] + side_in[0, c] + side_in[1, c]
            ).astype(BF16)

    def end_ring():
        for c in order:
            relay_copy(c).wait_send()
            up_copy(c).wait_send()
            down_copy(c).wait_send()

    phases = (
        (run_maps, end_maps),
        (run_reads, None),
        (run_gather, None),
        (run_compose, None),
        (run_lines, end_lines),
        (run_starts, end_starts),
        (run_gated, None),
        (run_project, end_pair),
        (run_pair, None),
        (run_ring, end_ring),
    )
    for run, end in phases:
        run()
    for run, end in phases:
        if end is not None:
            end()


def on_device(queries, key_vecs, values, out_gate, beta_rates, log_decay, norm_gain, w_out):
    inner, outer = w_out.shape
    width = outer // CHUNKS
    vmem = pl.BlockSpec(memory_space=pltpu.VMEM)
    dma = pltpu.SemaphoreType.DMA
    square = (W, W)
    return pl.pallas_call(
        layer_kernel,
        name="layer",
        out_shape=jax.ShapeDtypeStruct((16, outer), BF16),
        in_specs=[vmem] * 7 + [pl.BlockSpec(memory_space=pl.ANY)],
        out_specs=vmem,
        scratch_shapes=[
            pltpu.VMEM((inner, outer), BF16),
            pltpu.VMEM((MICRO, inner), BF16),
            pltpu.VMEM((MICRO, inner), BF16),
            pltpu.VMEM((HEADS, 2) + square, F32),
            pltpu.VMEM((HEADS, 2 * MICRO, 4 * W), BF16),
            pltpu.VMEM((HEADS,) + square, F32),
            pltpu.VMEM((HEADS, W, 2 * W), BF16),
            pltpu.VMEM((W, inner), F32),
            pltpu.VMEM((LINE, 2) + square, F32),
            pltpu.VMEM((LINE * W, 2 * W), BF16),
            pltpu.VMEM((LINE,) + square, F32),
            pltpu.VMEM((2,) + square, F32),
            pltpu.VMEM((2,) + square, F32),
            pltpu.VMEM(square, F32),
            pltpu.VMEM(square, F32),
            pltpu.VMEM((LINE,) + square, F32),
            pltpu.VMEM((HEADS,) + square, F32),
            pltpu.VMEM((2 * RING, 16, inner), BF16),
            pltpu.VMEM((CHUNKS, RING, 16, width), F32),
            pltpu.VMEM((CHUNKS, RING, 16, width), F32),
            pltpu.VMEM((CHUNKS, RING, 16, width), F32),
            pltpu.VMEM((CHUNKS, 16, width), F32),
            pltpu.VMEM((2, CHUNKS, 16, width), F32),
            dma,
            dma((HEADS,)),
            dma((LINE,)),
            dma((2,)),
            dma((2,)),
            dma((LINE,)),
            dma((HEADS,)),
            dma((CHUNKS,)),
            dma((CHUNKS,)),
            dma((3, CHUNKS)),
            dma((3, CHUNKS)),
        ],
        compiler_params=pltpu.CompilerParams(
            collective_id=0, has_side_effects=True, vmem_limit_bytes=56 * 1024 * 1024
        ),
    )(
        queries,
        key_vecs.transpose(1, 0, 2),
        values.transpose(1, 0, 2),
        out_gate,
        beta_rates,
        log_decay,
        norm_gain.reshape(1, W),
        w_out,
    )


def solution(mesh):
    placed = (
        P("seq", "head"),
        P("seq", None, "head"),
        P("seq", None, "head"),
        P("seq", "head"),
        P(None, "head", "seq"),
        P("head", "seq"),
        P(),
        P("head", None),
    )
    return jax.shard_map(
        on_device, mesh=mesh, in_specs=placed, out_specs=P(("seq", "head"), None), check_vma=False
    )
```

```python
import functools

import jax
import jax.numpy as jnp
from jax import lax
from jax.experimental import pallas as pl
from jax.experimental.pallas import tpu as pltpu
from jax.sharding import PartitionSpec as P

F32 = jnp.float32
BF16 = jnp.bfloat16
EXACT = lax.Precision.HIGHEST
W = 128
STEPS = 3
MICRO = STEPS * W
HEADS = 4
GROUP = 4
BASE = 32
LINE = 8
ROWS = 4
RING = 4
CHUNKS = 4
MESH = pl.DeviceIdType.MESH


def iota(shape, dim):
    return lax.broadcasted_iota(jnp.int32, shape, dim)


def split(a):
    hi = a.astype(BF16)
    return hi, (a - hi.astype(F32)).astype(BF16)


def lhs_of(a):
    return jnp.concatenate(split(a), axis=1)


def rhs_of(b):
    pair = jnp.concatenate(split(b), axis=1)
    return jnp.concatenate([pair, pair], axis=0)


def mm(left, right):
    out = jnp.dot(left, right, preferred_element_type=F32)
    half = out.shape[1] // 2
    return out[:, :half] + out[:, half:]


def nt(a, b, precision=None):
    return lax.dot_general(
        a, b, (((1,), (1,)), ((), ())), preferred_element_type=F32, precision=precision
    )


def local_maps(k_ref, v_ref, beta_ref, decay_ref, tf_ref, x_ref, emit):
    step_i, token_i = iota((MICRO, W), 0), iota((MICRO, W), 1)
    upto = (STEPS * token_i <= step_i).astype(F32)
    decay = jnp.maximum(decay_ref[...], -110.0)
    g_col = nt(upto, decay, EXACT)
    g_row = nt(decay, upto, EXACT)
    b_col = sum(
        nt((STEPS * token_i + j == step_i).astype(F32), beta_ref[j], EXACT) for j in range(STEPS)
    )
    row_i, col_i = iota((W, W), 0), iota((W, W), 1)
    strict = row_i > col_i
    eye = (row_i == col_i).astype(F32)
    ones = jnp.ones((8, 2 * W), BF16)
    lane_block = iota((BASE, W), 1) // BASE
    r_cols, r_rows, systems, packed = [], [], [], []
    for h in range(HEADS):
        keys = k_ref[:, h * W : (h + 1) * W]
        wide = keys.astype(F32)
        squares = wide * wide
        r_c = 1.0 / jnp.sqrt(jnp.sum(squares, axis=1, keepdims=True) + 1e-6)
        r_r = 1.0 / jnp.sqrt(nt(ones, lhs_of(squares))[0:1] + 1e-6)
        r_cols.append(r_c)
        r_rows.append(r_r)
        scale = b_col[:, h : h + 1] * r_c
        blocks = {}
        for i in range(3):
            for j in range(i + 1):
                si, sj = slice(i * W, (i + 1) * W), slice(j * W, (j + 1) * W)
                gap = g_col[si, h : h + 1] - g_row[h : h + 1, sj]
                if i == j:
                    gap = jnp.where(strict, gap, 0.0)
                a = nt(keys[si], keys[sj]) * (scale[si] * r_r[:, sj]) * jnp.exp(gap)
                if i == j:
                    a = jnp.where(strict, a, 0.0)
                    packed.append(
                        sum(
                            jnp.where(lane_block == b, a[b * BASE : (b + 1) * BASE], 0.0)
                            for b in range(W // BASE)
                        )
                    )
                blocks[i, j] = a
        systems.append(blocks)
    count = len(packed)
    packed = lhs_of(jnp.concatenate(packed, axis=0))
    block_start = (col_i // BASE) * BASE
    small = [
        (iota((count, 8, W), 1) + 8 * s == iota((count, 8, W), 2) % BASE).astype(F32)
        for s in range(BASE // 8)
    ]
    for j in range(BASE - 1):
        pick = (row_i == block_start + j).astype(BF16)
        factor = jnp.dot(
            packed, jnp.concatenate([pick, pick], axis=0), preferred_element_type=F32
        ).reshape(count, BASE, W)
        first = j // 8
        row = small[first][:, j % 8 : j % 8 + 1, :]
        for s in range(first, BASE // 8):
            small[s] = small[s] - factor[:, 8 * s : 8 * s + 8, :] * row
    same32 = (row_i // 32) == (col_i // 32)
    same64 = (row_i // 64) == (col_i // 64)
    low32 = same64 & jnp.logical_not(same32)
    low64 = jnp.logical_not(same64)
    for group in range(0, HEADS, GROUP):
        heads = range(group, group + GROUP)
        inverse = {}
        for h in heads:
            for i in range(3):
                n = h * 3 + i
                tile = jnp.concatenate([small[s][n] for s in range(BASE // 8)], axis=0)
                inverse[h, i] = jnp.where(same32, jnp.concatenate([tile] * (W // BASE), axis=0), 0.0)
        for low in (low32, low64):
            step = {
                n: mm(lhs_of(inv), rhs_of(jnp.where(low, systems[n[0]][n[1], n[1]], 0.0)))
                for n, inv in inverse.items()
            }
            inverse = {n: inv - mm(lhs_of(step[n]), rhs_of(inv)) for n, inv in inverse.items()}
        wide, right, x1, x1r, x2, x3, solved = {}, {}, {}, {}, {}, {}, {}
        for h in heads:
            b_c, g_c = b_col[:, h : h + 1], g_col[:, h : h + 1]
            wide[h] = k_ref[:, h * W : (h + 1) * W].astype(F32)
            right[h] = jnp.concatenate(
                [
                    b_c * v_ref[:, h * W : (h + 1) * W].astype(F32),
                    (b_c * jnp.exp(g_c) * r_cols[h]) * wide[h],
                ],
                axis=1,
            )
        for h in heads:
            x1[h] = mm(lhs_of(inverse[h, 0]), rhs_of(right[h][:W]))
        for h in heads:
            x1r[h] = rhs_of(x1[h])
            x2[h] = right[h][W : 2 * W] - mm(lhs_of(systems[h][1, 0]), x1r[h])
        for h in heads:
            x2[h] = mm(lhs_of(inverse[h, 1]), rhs_of(x2[h]))
        for h in heads:
            x3[h] = right[h][2 * W :] - mm(lhs_of(systems[h][2, 0]), x1r[h])
        for h in heads:
            x3[h] = x3[h] - mm(lhs_of(systems[h][2, 1]), rhs_of(x2[h]))
        for h in heads:
            x3[h] = mm(lhs_of(inverse[h, 2]), rhs_of(x3[h]))
        for h in heads:
            solved = jnp.concatenate([x1[h], x2[h], x3[h]], axis=0)
            x_ref[h] = rhs_of(solved)
            g_c, g_end = g_col[:, h : h + 1], g_col[MICRO - 1 : MICRO, h : h + 1]
            tail = jnp.concatenate(split((r_cols[h] * jnp.exp(g_end - g_c)) * solved), axis=1)
            out = jnp.dot(wide[h].T.astype(BF16), tail, preferred_element_type=F32)
            out = out[:, : 2 * W] + out[:, 2 * W :]
            tf_ref[h, 0] = jnp.exp(g_end) * eye - out[:, W:]
            tf_ref[h, 1] = out[:, :W]
        for h in heads:
            emit(h)
    return g_row, r_rows


def local_reads(q_ref, k_ref, decay_ref, x_ref, g_row, r_rows, lo_ref, lq_ref):
    decay = jnp.maximum(decay_ref[...], -110.0)
    upto = (iota((W, W), 1) <= iota((W, W), 0)).astype(F32)
    q_col = nt(upto, decay, EXACT)
    visible = iota((W, MICRO), 1) <= STEPS * iota((W, MICRO), 0) + STEPS - 1
    heads = range(HEADS)
    query = [q_ref[:, h * W : (h + 1) * W] for h in heads]
    scores = [nt(query[h], k_ref[:, h * W : (h + 1) * W]) for h in heads]
    gaps = [jnp.where(visible, q_col[:, h : h + 1] - g_row[h : h + 1, :], 0.0) for h in heads]
    scores = [jnp.where(visible, scores[h] * (r_rows[h] * jnp.exp(gaps[h])), 0.0) for h in heads]
    reads = [mm(lhs_of(scores[h]), x_ref[h]) for h in heads]
    for h in heads:
        lo_ref[h] = reads[h][:, :W]
        lq_ref[h] = lhs_of(jnp.exp(q_col[:, h : h + 1]) * query[h].astype(F32) - reads[h][:, W:])


def compose(lefts, right):
    out = mm(
        jnp.concatenate([lhs_of(t) for t, f in lefts], axis=0),
        rhs_of(jnp.concatenate(right, axis=1)),
    )
    return [
        (out[i * W : (i + 1) * W, :W], out[i * W : (i + 1) * W, W:] + lefts[i][1])
        for i in range(len(lefts))
    ]


def layer_kernel(
    q_ref, k_ref, v_ref, gate_ref, beta_ref, decay_ref, gain_ref, w_hbm, out_ref,
    w_ref, keys_ref, values_ref, tf_ref, x_ref, lo_ref, lq_ref, act_ref,
    maps_ref, pre_t_ref, pre_f_ref, total_ref, far_ref, line_ref, next_ref, given_ref, start_ref,
    gated_ref, pair_out, pair_in, own_ref, relay_in, side_in,
    w_sem, map_send, map_recv, line_send, line_recv, start_send, start_recv,
    pair_send, pair_recv, ring_send, ring_recv,
):
    seq, head = lax.axis_index("seq"), lax.axis_index("head")
    x, z = seq // LINE, lax.rem(seq, LINE)
    y, core = head // 2, lax.rem(head, 2)
    line = x * LINE
    owner = core == 1
    mine, mine_core = z // 2, lax.rem(z, 2)
    width = w_ref.shape[1] // CHUNKS
    order = (0, 2, 1, 3)
    held = {}

    def at(s, h):
        return {"device_id": (s, h), "device_id_type": MESH}

    owners, served = y * 2 + 1, y * 2 + mine_core
    up = lax.rem(y + 1, RING) * 2 + core
    down = lax.rem(y + RING - 1, RING) * 2 + core
    sibling = y * 2 + 1 - core

    w_copy = pltpu.make_async_copy(w_hbm, w_ref, w_sem)
    w_copy.start()

    barrier = pltpu.get_barrier_semaphore()
    for i in range(1, LINE):
        for h in (head, sibling):
            pl.semaphore_signal(barrier, inc=1, **at(line + lax.rem(z + i, LINE), h))
    for i in range(1, ROWS):
        pl.semaphore_signal(barrier, inc=1, **at(lax.rem(x + i, ROWS) * LINE + z, head))
    for h in (up, down, sibling):
        pl.semaphore_signal(barrier, inc=1, **at(seq, h))

    def map_copy(h):
        return pltpu.make_async_remote_copy(
            src_ref=tf_ref.at[h], dst_ref=maps_ref.at[z],
            send_sem=map_send.at[h], recv_sem=map_recv.at[z],
            **at(line + 2 * h + core, owners),
        )

    def line_copy(src, dst, send, recv, to):
        return pltpu.make_async_remote_copy(
            src_ref=src, dst_ref=dst, send_sem=line_send.at[send], recv_sem=line_recv.at[recv],
            **at(to * LINE + z, head),
        )

    def start_copy(to, h):
        return pltpu.make_async_remote_copy(
            src_ref=given_ref.at[to], dst_ref=start_ref.at[h],
            send_sem=start_send.at[to], recv_sem=start_recv.at[h], **at(line + to, served),
        )

    def pair_copy(c):
        return pltpu.make_async_remote_copy(
            src_ref=pair_out.at[c], dst_ref=pair_in.at[c],
            send_sem=pair_send.at[c], recv_sem=pair_recv.at[c], **at(seq, sibling),
        )

    def ring_copy(kind, c, src, dst, to):
        return pltpu.make_async_remote_copy(
            src_ref=src, dst_ref=dst, send_sem=ring_send.at[kind, c], recv_sem=ring_recv.at[kind, c],
            **at(seq, to),
        )

    def relay_copy(c):
        return ring_copy(0, c, own_ref.at[c, 2], relay_in.at[c], up if c < 2 else down)

    def up_copy(c):
        return ring_copy(1, c, own_ref.at[c, 1], side_in.at[0, c], up)

    def down_copy(c):
        return ring_copy(2, c, own_ref.at[c, 3], side_in.at[1, c], down)

    def run_maps():
        to_time = (STEPS * lax.rem(iota((MICRO, MICRO), 1), W) + iota((MICRO, MICRO), 1) // W == iota((MICRO, MICRO), 0)).astype(BF16)
        for src, dst in ((k_ref, keys_ref), (v_ref, values_ref)):
            flat = src[...].reshape(MICRO, HEADS * W)
            dst[...] = jnp.dot(to_time, flat, preferred_element_type=F32).astype(BF16)

        def emit(h):
            if h == 0:
                pl.semaphore_wait(barrier, 2 * (LINE - 1) + ROWS - 1 + 3)

            keep = owner & (z == 2 * h + 1)

            @pl.when(jnp.logical_not(keep))
            def _():
                map_copy(h).start()

            @pl.when(keep)
            def _():
                maps_ref[z] = tf_ref[h]

        held["rows"] = local_maps(keys_ref, values_ref, beta_ref, decay_ref, tf_ref, x_ref, emit)

    def end_maps():
        for h in range(HEADS):
            @pl.when(jnp.logical_not(owner & (z == 2 * h + 1)))
            def _():
                map_copy(h).wait_send()

    def run_reads():
        g_row, r_rows = held["rows"]
        local_reads(q_ref, keys_ref, decay_ref, x_ref, g_row, r_rows, lo_ref, lq_ref)
        gate = gate_ref[...].astype(F32)
        act_ref[...] = (gate / (1.0 + jnp.exp(-gate))) * jnp.concatenate(
            [gain_ref[...]] * HEADS, axis=1
        )

    def run_gather():
        @pl.when(owner)
        def _():
            def arrived(other):
                pltpu.make_async_remote_copy(
                    src_ref=tf_ref.at[0], dst_ref=maps_ref.at[other],
                    send_sem=map_send.at[0], recv_sem=map_recv.at[other], **at(line + other, sibling),
                ).wait_recv()

            for i in range(1, LINE):
                arrived(lax.rem(z + i, LINE))

            @pl.when(mine_core == 0)
            def _():
                arrived(z)

    def run_compose():
        @pl.when(owner)
        def _():
            m = [(maps_ref[i, 0], maps_ref[i, 1]) for i in range(LINE)]
            (p1,) = compose([m[1]], m[0])
            (q23,) = compose([m[3]], m[2])
            (q45,) = compose([m[5]], m[4])
            (q67,) = compose([m[7]], m[6])
            p2, p3 = compose([m[2], q23], p1)
            q46, q47 = compose([m[6], q67], q45)
            p4, p5, p6, p7 = compose([m[4], q45, q46, q47], p3)
            total_ref[0] = p7[0]
            total_ref[1] = p7[1]
            for i, (t, f) in enumerate((m[0], p1, p2, p3, p4, p5, p6, p7)):
                pre_t_ref[i * W : (i + 1) * W] = lhs_of(t)
                pre_f_ref[i] = f

    def run_lines():
        @pl.when(owner)
        def _():
            @pl.when(x == 0)
            def _():
                line_copy(total_ref.at[1], line_ref, 0, 0, 1).start()
                given_ref[0] = jnp.zeros((W, W), F32)

            @pl.when(x == 2)
            def _():
                line_copy(total_ref, far_ref, 0, 1, 3).start()

            @pl.when(x == 1)
            def _():
                line_copy(total_ref.at[1], line_ref, 0, 0, 1).wait_recv()
                next_ref[...] = mm(pre_t_ref[7 * W :], rhs_of(line_ref[...])) + pre_f_ref[7]
                line_copy(next_ref, line_ref, 0, 0, 3).start()
                line_copy(next_ref, line_ref, 1, 0, 2).start()
                given_ref[0] = line_ref[...]

            @pl.when(x == 2)
            def _():
                line_copy(total_ref.at[1], line_ref, 0, 0, 1).wait_recv()
                given_ref[0] = line_ref[...]

            @pl.when(x == 3)
            def _():
                line_copy(total_ref, far_ref, 0, 1, 3).wait_recv()
                far = lhs_of(far_ref[0])
                line_copy(total_ref.at[1], line_ref, 0, 0, 1).wait_recv()
                given_ref[0] = mm(far, rhs_of(line_ref[...])) + far_ref[1]

    def end_lines():
        @pl.when(owner)
        def _():
            @pl.when(x == 0)
            def _():
                line_copy(total_ref.at[1], line_ref, 0, 0, 1).wait_send()

            @pl.when(x == 2)
            def _():
                line_copy(total_ref, far_ref, 0, 1, 3).wait_send()

            @pl.when(x == 1)
            def _():
                line_copy(next_ref, line_ref, 0, 0, 3).wait_send()
                line_copy(next_ref, line_ref, 1, 0, 2).wait_send()

    def run_starts():
        def give(to):
            keep = (z == to) & (mine_core == 1)

            @pl.when(jnp.logical_not(keep))
            def _():
                start_copy(to, mine).start()

            @pl.when(keep)
            def _():
                start_ref[mine] = given_ref[to]

        @pl.when(owner)
        def _():
            give(0)
            for batch in ((1, 2, 3, 7), (4, 5, 6)):
                @pl.when(x == 0)
                def _():
                    for to in batch:
                        given_ref[to] = pre_f_ref[to - 1]

                @pl.when(x > 0)
                def _():
                    begin = rhs_of(given_ref[0])
                    after = [mm(pre_t_ref[(to - 1) * W : to * W], begin) for to in batch]
                    for to, part in zip(batch, after):
                        given_ref[to] = part + pre_f_ref[to - 1]

                for to in batch:
                    give(to)

        for h in range(HEADS):
            @pl.when(jnp.logical_not(owner & (z == 2 * h + 1)))
            def _():
                start_copy(0, h).wait_recv()

    def end_starts():
        @pl.when(owner)
        def _():
            for to in range(LINE):
                @pl.when(jnp.logical_not((z == to) & (mine_core == 1)))
                def _():
                    start_copy(to, mine).wait_send()

    def run_gated():
        for h in range(HEADS):
            heads_out = lo_ref[h] + mm(lq_ref[h], rhs_of(start_ref[h]))
            mean = jnp.sum(heads_out * heads_out, axis=1, keepdims=True) * (1.0 / W)
            normed = heads_out / jnp.sqrt(mean + 1e-5)
            gated_ref[:, :, h * W : (h + 1) * W] = (
                (normed * act_ref[:, h * W : (h + 1) * W]).astype(BF16).reshape(2 * RING, 16, W)
            )

    def run_project():
        w_copy.wait()
        block = [lax.rem(y + i, RING) * 2 for i in range(RING)]
        rows = jnp.concatenate(
            [gated_ref[b + 1 - core] for b in block] + [gated_ref[b + core] for b in block], axis=0
        )
        for c in order:
            part = jnp.dot(rows, w_ref[:, c * width : (c + 1) * width], preferred_element_type=F32)
            pair_out[c] = part[:64].reshape(RING, 16, width)
            pair_copy(c).start()
            own_ref[c] = part[64:].reshape(RING, 16, width)

    def end_pair():
        for c in order:
            pair_copy(c).wait_send()

    def run_ring():
        for c in order:
            pair_copy(c).wait_recv()
            own_ref[c] = own_ref[c] + pair_in[c]
            relay_copy(c).start()
            (down_copy if c < 2 else up_copy)(c).start()
        for c in order:
            relay_copy(c).wait_recv()
            if c < 2:
                own_ref[c, 1] = own_ref[c, 1] + relay_in[c]
                up_copy(c).start()
            else:
                own_ref[c, 3] = own_ref[c, 3] + relay_in[c]
                down_copy(c).start()
        for c in order:
            up_copy(c).wait_recv()
            down_copy(c).wait_recv()
            out_ref[:, c * width : (c + 1) * width] = (
                own_ref[c, 0] + side_in[0, c] + side_in[1, c]
            ).astype(BF16)

    def end_ring():
        for c in order:
            relay_copy(c).wait_send()
            up_copy(c).wait_send()
            down_copy(c).wait_send()

    phases = (
        (run_maps, end_maps),
        (run_reads, None),
        (run_gather, None),
        (run_compose, None),
        (run_lines, end_lines),
        (run_starts, end_starts),
        (run_gated, None),
        (run_project, end_pair),
        (run_ring, end_ring),
    )
    for run, end in phases:
        run()
    for run, end in phases:
        if end is not None:
            end()


def on_device(queries, key_vecs, values, out_gate, beta_rates, log_decay, norm_gain, w_out):
    inner, outer = w_out.shape
    width = outer // CHUNKS
    vmem = pl.BlockSpec(memory_space=pltpu.VMEM)
    dma = pltpu.SemaphoreType.DMA
    square = (W, W)
    return pl.pallas_call(
        layer_kernel,
        name="layer",
        out_shape=jax.ShapeDtypeStruct((16, outer), BF16),
        in_specs=[vmem] * 7 + [pl.BlockSpec(memory_space=pl.ANY)],
        out_specs=vmem,
        scratch_shapes=[
            pltpu.VMEM((inner, outer), BF16),
            pltpu.VMEM((MICRO, inner), BF16),
            pltpu.VMEM((MICRO, inner), BF16),
            pltpu.VMEM((HEADS, 2) + square, F32),
            pltpu.VMEM((HEADS, 2 * MICRO, 4 * W), BF16),
            pltpu.VMEM((HEADS,) + square, F32),
            pltpu.VMEM((HEADS, W, 2 * W), BF16),
            pltpu.VMEM((W, inner), F32),
            pltpu.VMEM((LINE, 2) + square, F32),
            pltpu.VMEM((LINE * W, 2 * W), BF16),
            pltpu.VMEM((LINE,) + square, F32),
            pltpu.VMEM((2,) + square, F32),
            pltpu.VMEM((2,) + square, F32),
            pltpu.VMEM(square, F32),
            pltpu.VMEM(square, F32),
            pltpu.VMEM((LINE,) + square, F32),
            pltpu.VMEM((HEADS,) + square, F32),
            pltpu.VMEM((2 * RING, 16, inner), BF16),
            pltpu.VMEM((CHUNKS, RING, 16, width), F32),
            pltpu.VMEM((CHUNKS, RING, 16, width), F32),
            pltpu.VMEM((CHUNKS, RING, 16, width), F32),
            pltpu.VMEM((CHUNKS, 16, width), F32),
            pltpu.VMEM((2, CHUNKS, 16, width), F32),
            dma,
            dma((HEADS,)),
            dma((LINE,)),
            dma((2,)),
            dma((2,)),
            dma((LINE,)),
            dma((HEADS,)),
            dma((CHUNKS,)),
            dma((CHUNKS,)),
            dma((3, CHUNKS)),
            dma((3, CHUNKS)),
        ],
        compiler_params=pltpu.CompilerParams(
            collective_id=0, has_side_effects=True, vmem_limit_bytes=56 * 1024 * 1024
        ),
    )(
        queries,
        key_vecs.transpose(1, 0, 2),
        values.transpose(1, 0, 2),
        out_gate,
        beta_rates,
        log_decay,
        norm_gain.reshape(1, W),
        w_out,
    )


def solution(mesh):
    placed = (
        P("seq", "head"),
        P("seq", None, "head"),
        P("seq", None, "head"),
        P("seq", "head"),
        P(None, "head", "seq"),
        P("head", "seq"),
        P(),
        P("head", None),
    )
    return jax.shard_map(
        on_device, mesh=mesh, in_specs=placed, out_specs=P(("seq", "head"), None), check_vma=False
    )
```

```python
import functools

import jax
import jax.numpy as jnp
from jax import lax
from jax.experimental import pallas as pl
from jax.experimental.pallas import tpu as pltpu
from jax.sharding import PartitionSpec as P

F32 = jnp.float32
BF16 = jnp.bfloat16
W = 128
STEPS = 3
MICRO = STEPS * W
HEADS = 4
GROUP = 4
BASE = 16
LINE = 8
ROWS = 4
RING = 4
CHUNKS = 4
MESH = pl.DeviceIdType.MESH


def iota(shape, dim):
    return lax.broadcasted_iota(jnp.int32, shape, dim)


def split(a):
    hi = a.astype(BF16)
    return hi, (a - hi.astype(F32)).astype(BF16)


def split3(a):
    hi, rest = a.astype(BF16), a - a.astype(BF16).astype(F32)
    return (hi,) + split(rest)


def lhs_of(a):
    return jnp.concatenate(split(a), axis=1)


def rhs_of(b):
    pair = jnp.concatenate(split(b), axis=1)
    return jnp.concatenate([pair, pair], axis=0)


def mm(left, right):
    out = jnp.dot(left, right, preferred_element_type=F32)
    half = out.shape[1] // 2
    return out[:, :half] + out[:, half:]


def nt(a, b):
    return lax.dot_general(a, b, (((1,), (1,)), ((), ())), preferred_element_type=F32)


def local_maps(raw_ref, v_ref, beta_ref, decay_ref, k_ref, tf_ref, x_ref, v_wait):
    time_i, flat_i = iota((MICRO, MICRO), 0), iota((MICRO, MICRO), 1)
    to_time = (STEPS * lax.rem(flat_i, W) + flat_i // W == time_i).astype(BF16)
    raw = raw_ref[...].reshape(MICRO, HEADS * W)
    k_ref[...] = jnp.dot(to_time, raw, preferred_element_type=F32).astype(BF16)
    upto = (STEPS * iota((MICRO, W), 1) <= iota((MICRO, W), 0)).astype(BF16)
    upto = jnp.concatenate([upto] * 3, axis=1)
    decay = jnp.concatenate(split3(jnp.maximum(decay_ref[...], -110.0)), axis=1)
    g_col = nt(upto, decay)
    g_row = nt(decay, upto)
    beta = jnp.concatenate([beta_ref[j] for j in range(STEPS)], axis=1)
    b_col = nt(jnp.concatenate([to_time] * 3, axis=1), jnp.concatenate(split3(beta), axis=1))
    row_i, col_i = iota((W, W), 0), iota((W, W), 1)
    strict = row_i > col_i
    eye = (row_i == col_i).astype(F32)
    ones = jnp.ones((8, 2 * W), BF16)
    lane_block = iota((BASE, W), 1) // BASE
    r_cols, r_rows, systems, packed = [], [], [], []
    for h in range(HEADS):
        keys = k_ref[:, h * W : (h + 1) * W]
        wide = keys.astype(F32)
        squares = wide * wide
        r_c = 1.0 / jnp.sqrt(jnp.sum(squares, axis=1, keepdims=True) + 1e-6)
        r_r = 1.0 / jnp.sqrt(nt(ones, lhs_of(squares))[0:1] + 1e-6)
        r_cols.append(r_c)
        r_rows.append(r_r)
        scale = b_col[:, h : h + 1] * r_c
        blocks = {}
        for i in range(3):
            for j in range(i + 1):
                si, sj = slice(i * W, (i + 1) * W), slice(j * W, (j + 1) * W)
                gap = g_col[si, h : h + 1] - g_row[h : h + 1, sj]
                if i == j:
                    gap = jnp.where(strict, gap, 0.0)
                a = nt(keys[si], keys[sj]) * (scale[si] * r_r[:, sj]) * jnp.exp(gap)
                if i == j:
                    a = jnp.where(strict, a, 0.0)
                    packed.append(
                        sum(
                            jnp.where(lane_block == b, a[b * BASE : (b + 1) * BASE], 0.0)
                            for b in range(W // BASE)
                        )
                    )
                blocks[i, j] = a
        systems.append(blocks)
    count = len(packed)
    packed = lhs_of(jnp.concatenate(packed, axis=0))
    block_start = (col_i // BASE) * BASE
    small = [
        (iota((count, 8, W), 1) + 8 * s == iota((count, 8, W), 2) % BASE).astype(F32)
        for s in range(BASE // 8)
    ]
    for j in range(BASE - 1):
        pick = (row_i == block_start + j).astype(BF16)
        factor = jnp.dot(
            packed, jnp.concatenate([pick, pick], axis=0), preferred_element_type=F32
        ).reshape(count, BASE, W)
        first = j // 8
        row = small[first][:, j % 8 : j % 8 + 1, :]
        for s in range(first, BASE // 8):
            small[s] = small[s] - factor[:, 8 * s : 8 * s + 8, :] * row
    same = {n: (row_i // n) == (col_i // n) for n in (16, 32, 64)}
    lows = {
        16: same[32] & jnp.logical_not(same[16]),
        32: same[64] & jnp.logical_not(same[32]),
        64: jnp.logical_not(same[64]),
    }
    for group in range(0, HEADS, GROUP):
        heads = range(group, group + GROUP)
        inverse = {}
        for h in heads:
            for i in range(3):
                n = h * 3 + i
                tile = jnp.concatenate([small[s][n] for s in range(BASE // 8)], axis=0)
                inverse[h, i] = jnp.where(same[BASE], jnp.concatenate([tile] * (W // BASE), axis=0), 0.0)
        for low in [lows[n] for n in (16, 32, 64) if n >= BASE]:
            step = {
                n: mm(lhs_of(inv), rhs_of(jnp.where(low, systems[n[0]][n[1], n[1]], 0.0)))
                for n, inv in inverse.items()
            }
            inverse = {n: inv - mm(lhs_of(step[n]), rhs_of(inv)) for n, inv in inverse.items()}
        v_wait()
        wide, right, x1, x1r, x2, x3, solved = {}, {}, {}, {}, {}, {}, {}
        values = v_ref[...].reshape(MICRO, HEADS * W)
        values = jnp.dot(to_time, values, preferred_element_type=F32)
        for h in heads:
            b_c, g_c = b_col[:, h : h + 1], g_col[:, h : h + 1]
            wide[h] = k_ref[:, h * W : (h + 1) * W].astype(F32)
            right[h] = jnp.concatenate(
                [
                    b_c * values[:, h * W : (h + 1) * W],
                    (b_c * jnp.exp(g_c) * r_cols[h]) * wide[h],
                ],
                axis=1,
            )
        for h in heads:
            x1[h] = mm(lhs_of(inverse[h, 0]), rhs_of(right[h][:W]))
        for h in heads:
            x1r[h] = rhs_of(x1[h])
            x2[h] = right[h][W : 2 * W] - mm(lhs_of(systems[h][1, 0]), x1r[h])
        for h in heads:
            x2[h] = mm(lhs_of(inverse[h, 1]), rhs_of(x2[h]))
        for h in heads:
            x3[h] = right[h][2 * W :] - mm(lhs_of(systems[h][2, 0]), x1r[h])
        for h in heads:
            x3[h] = x3[h] - mm(lhs_of(systems[h][2, 1]), rhs_of(x2[h]))
        for h in heads:
            x3[h] = mm(lhs_of(inverse[h, 2]), rhs_of(x3[h]))
        for h in heads:
            solved = jnp.concatenate([x1[h], x2[h], x3[h]], axis=0)
            x_ref[h] = rhs_of(solved)
            g_c, g_end = g_col[:, h : h + 1], g_col[MICRO - 1 : MICRO, h : h + 1]
            tail = jnp.concatenate(split((r_cols[h] * jnp.exp(g_end - g_c)) * solved), axis=1)
            out = jnp.dot(wide[h].T.astype(BF16), tail, preferred_element_type=F32)
            out = out[:, : 2 * W] + out[:, 2 * W :]
            tf_ref[h, 0] = jnp.exp(g_end) * eye - out[:, W:]
            tf_ref[h, 1] = out[:, :W]
    return g_row, r_rows


def local_reads(q_ref, k_ref, decay_ref, x_ref, g_row, r_rows, lo_ref, lq_ref):
    decay = jnp.concatenate(split3(jnp.maximum(decay_ref[...], -110.0)), axis=1)
    upto = (iota((W, W), 1) <= iota((W, W), 0)).astype(BF16)
    q_col = nt(jnp.concatenate([upto] * 3, axis=1), decay)
    visible = iota((W, MICRO), 1) <= STEPS * iota((W, MICRO), 0) + STEPS - 1
    heads = range(HEADS)
    query = [q_ref[:, h * W : (h + 1) * W] for h in heads]
    scores = [nt(query[h], k_ref[:, h * W : (h + 1) * W]) for h in heads]
    gaps = [jnp.where(visible, q_col[:, h : h + 1] - g_row[h : h + 1, :], 0.0) for h in heads]
    scores = [jnp.where(visible, scores[h] * (r_rows[h] * jnp.exp(gaps[h])), 0.0) for h in heads]
    reads = [mm(lhs_of(scores[h]), x_ref[h]) for h in heads]
    for h in heads:
        lo_ref[h] = reads[h][:, :W]
        lq_ref[h] = lhs_of(jnp.exp(q_col[:, h : h + 1]) * query[h].astype(F32) - reads[h][:, W:])


def compose(lefts, right):
    out = mm(
        jnp.concatenate([lhs_of(t) for t, f in lefts], axis=0),
        rhs_of(jnp.concatenate(right, axis=1)),
    )
    return [
        (out[i * W : (i + 1) * W, :W], out[i * W : (i + 1) * W, W:] + lefts[i][1])
        for i in range(len(lefts))
    ]


def layer_kernel(
    q_hbm, k_hbm, v_hbm, gate_hbm, beta_ref, decay_ref, gain_ref, w_hbm, out_ref,
    q_ref, raw_ref, v_ref, gate_ref, w_ref, keys_ref, tf_ref, x_ref, lo_ref, lq_ref, act_ref,
    maps_ref, pre_t_ref, pre_f_ref, total_ref, far_ref, line_ref, given_ref, start_ref,
    gated_ref, pair_out, pair_in, own_ref, relay_in, side_in,
    in_sem, w_sem, map_send, map_recv, line_send, line_recv, start_send, start_recv,
    pair_send, pair_recv, ring_send, ring_recv,
):
    seq, head = lax.axis_index("seq"), lax.axis_index("head")
    x, z = seq // LINE, lax.rem(seq, LINE)
    y, core = head // 2, lax.rem(head, 2)
    line = x * LINE
    owner = core == 1
    mine, mine_core = z // 2, lax.rem(z, 2)
    width = w_ref.shape[1] // CHUNKS
    held = {}

    def at(s, h):
        return {"device_id": (s, h), "device_id_type": MESH}

    owners, served = y * 2 + 1, y * 2 + mine_core
    up = lax.rem(y + 1, RING) * 2 + core
    down = lax.rem(y + RING - 1, RING) * 2 + core
    sibling = y * 2 + 1 - core

    inputs = ((k_hbm, raw_ref), (v_hbm, v_ref), (q_hbm, q_ref), (gate_hbm, gate_ref))

    def in_copy(i):
        return pltpu.make_async_copy(*inputs[i], in_sem.at[i])

    for i in range(4):
        in_copy(i).start()
    w_copy = pltpu.make_async_copy(w_hbm, w_ref, w_sem)

    barrier = pltpu.get_barrier_semaphore()
    for i in range(1, LINE):
        for h in (head, sibling):
            pl.semaphore_signal(barrier, inc=1, **at(line + lax.rem(z + i, LINE), h))
    for i in range(1, ROWS):
        pl.semaphore_signal(barrier, inc=1, **at(lax.rem(x + i, ROWS) * LINE + z, head))
    for h in (up, down, sibling):
        pl.semaphore_signal(barrier, inc=1, **at(seq, h))

    def map_copy(h):
        return pltpu.make_async_remote_copy(
            src_ref=tf_ref.at[h], dst_ref=maps_ref.at[z],
            send_sem=map_send.at[h], recv_sem=map_recv.at[z],
            **at(line + 2 * h + core, owners),
        )

    def line_copy(src, dst, send, recv, to):
        return pltpu.make_async_remote_copy(
            src_ref=src, dst_ref=dst, send_sem=line_send.at[send], recv_sem=line_recv.at[recv],
            **at(to * LINE + z, head),
        )

    def start_copy(to, h):
        return pltpu.make_async_remote_copy(
            src_ref=given_ref.at[to], dst_ref=start_ref.at[h],
            send_sem=start_send.at[to], recv_sem=start_recv.at[h], **at(line + to, served),
        )

    def pair_copy(c):
        return pltpu.make_async_remote_copy(
            src_ref=pair_out.at[c], dst_ref=pair_in.at[c],
            send_sem=pair_send.at[c], recv_sem=pair_recv.at[c], **at(seq, sibling),
        )

    def ring_copy(kind, c, src, dst, upward):
        return pltpu.make_async_remote_copy(
            src_ref=src, dst_ref=dst, send_sem=ring_send.at[kind, c], recv_sem=ring_recv.at[kind, c],
            **at(seq, jnp.where(upward, up, down)),
        )

    def relay_copy(c):
        return ring_copy(0, c, own_ref.at[c, 2], relay_in.at[c], c < CHUNKS // 2)

    def side_copy(c):
        part = c // (CHUNKS // 2)
        return ring_copy(1, c, own_ref.at[c, 3 - 2 * part], side_in.at[1 - part, c], part == 1)

    def onward_copy(c):
        part = c // (CHUNKS // 2)
        return ring_copy(2, c, own_ref.at[c, 1 + 2 * part], side_in.at[part, c], part == 0)

    def each_chunk(body):
        def step(i, carry):
            body(lax.rem(i, 2) * (CHUNKS // 2) + i // 2)
            return carry

        lax.fori_loop(0, CHUNKS, step, 0)

    def run_maps():
        in_copy(0).wait()
        held["rows"] = local_maps(
            raw_ref, v_ref, beta_ref, decay_ref, keys_ref, tf_ref, x_ref, in_copy(1).wait
        )
        pl.semaphore_wait(barrier, 2 * (LINE - 1) + ROWS - 1 + 3)
        for h in range(HEADS):
            keep = owner & (z == 2 * h + 1)

            @pl.when(jnp.logical_not(keep))
            def _():
                map_copy(h).start()

            @pl.when(keep)
            def _():
                maps_ref[z] = tf_ref[h]

    def end_maps():
        for h in range(HEADS):
            @pl.when(jnp.logical_not(owner & (z == 2 * h + 1)))
            def _():
                map_copy(h).wait_send()

    def run_reads():
        g_row, r_rows = held["rows"]
        in_copy(2).wait()
        in_copy(3).wait()
        local_reads(q_ref, keys_ref, decay_ref, x_ref, g_row, r_rows, lo_ref, lq_ref)
        gate = gate_ref[...].astype(F32)
        act_ref[...] = (gate / (1.0 + jnp.exp(-gate))) * jnp.concatenate(
            [gain_ref[...]] * HEADS, axis=1
        )

    def run_gather():
        @pl.when(owner)
        def _():
            def arrived(other):
                pltpu.make_async_remote_copy(
                    src_ref=tf_ref.at[0], dst_ref=maps_ref.at[other],
                    send_sem=map_send.at[0], recv_sem=map_recv.at[other], **at(line + other, sibling),
                ).wait_recv()

            for i in range(1, LINE):
                arrived(lax.rem(z + i, LINE))

            @pl.when(mine_core == 0)
            def _():
                arrived(z)

    def run_compose():
        @pl.when(owner)
        def _():
            m = [(maps_ref[i, 0], maps_ref[i, 1]) for i in range(LINE)]
            (p1,) = compose([m[1]], m[0])
            (q23,) = compose([m[3]], m[2])
            (q45,) = compose([m[5]], m[4])
            (q67,) = compose([m[7]], m[6])
            p2, p3 = compose([m[2], q23], p1)
            q46, q47 = compose([m[6], q67], q45)
            p4, p5, p6, p7 = compose([m[4], q45, q46, q47], p3)
            total_ref[0] = p7[0]
            total_ref[1] = p7[1]
            for i, (t, f) in enumerate((m[0], p1, p2, p3, p4, p5, p6, p7)):
                pre_t_ref[i * W : (i + 1) * W] = lhs_of(t)
                pre_f_ref[i] = f

    def run_weights():
        w_copy.start()

    def run_lines():
        @pl.when(owner)
        def _():
            @pl.when(x == 0)
            def _():
                for i, to in enumerate((3, 1, 2)):
                    line_copy(total_ref.at[1], line_ref, i, 0, to).start()
                given_ref[0] = jnp.zeros((W, W), F32)

            @pl.when(x == 1)
            def _():
                for i, to in enumerate((3, 2)):
                    line_copy(total_ref, far_ref.at[0], i, 1, to).start()

            @pl.when(x == 2)
            def _():
                line_copy(total_ref, far_ref.at[1], 0, 2, 3).start()

            @pl.when(x > 0)
            def _():
                line_copy(total_ref.at[1], line_ref, 0, 0, 1).wait_recv()
                given_ref[0] = line_ref[...]

            @pl.when(x > 1)
            def _():
                begin = rhs_of(line_ref[...])
                line_copy(total_ref, far_ref.at[0], 0, 1, 3).wait_recv()
                given_ref[0] = mm(lhs_of(far_ref[0, 0]), begin) + far_ref[0, 1]

            @pl.when(x == 3)
            def _():
                line_copy(total_ref, far_ref.at[1], 0, 2, 3).wait_recv()
                given_ref[0] = mm(lhs_of(far_ref[1, 0]), rhs_of(given_ref[0])) + far_ref[1, 1]

    def end_lines():
        @pl.when(owner)
        def _():
            @pl.when(x == 0)
            def _():
                for i, to in enumerate((3, 1, 2)):
                    line_copy(total_ref.at[1], line_ref, i, 0, to).wait_send()

            @pl.when(x == 1)
            def _():
                for i, to in enumerate((3, 2)):
                    line_copy(total_ref, far_ref.at[0], i, 1, to).wait_send()

            @pl.when(x == 2)
            def _():
                line_copy(total_ref, far_ref.at[1], 0, 2, 3).wait_send()

    def run_starts():
        def give(to):
            keep = (z == to) & (mine_core == 1)

            @pl.when(jnp.logical_not(keep))
            def _():
                start_copy(to, mine).start()

            @pl.when(keep)
            def _():
                start_ref[mine] = given_ref[to]

        @pl.when(owner)
        def _():
            give(0)
            for batch in ((1, 2, 3, 7), (4, 5, 6)):
                @pl.when(x == 0)
                def _():
                    for to in batch:
                        given_ref[to] = pre_f_ref[to - 1]

                @pl.when(x > 0)
                def _():
                    begin = rhs_of(given_ref[0])
                    after = [mm(pre_t_ref[(to - 1) * W : to * W], begin) for to in batch]
                    for to, part in zip(batch, after):
                        given_ref[to] = part + pre_f_ref[to - 1]

                for to in batch:
                    give(to)

        for h in range(HEADS):
            @pl.when(jnp.logical_not(owner & (z == 2 * h + 1)))
            def _():
                start_copy(0, h).wait_recv()

    def end_starts():
        @pl.when(owner)
        def _():
            for to in range(LINE):
                @pl.when(jnp.logical_not((z == to) & (mine_core == 1)))
                def _():
                    start_copy(to, mine).wait_send()

    def run_gated():
        for h in range(HEADS):
            heads_out = lo_ref[h] + mm(lq_ref[h], rhs_of(start_ref[h]))
            mean = jnp.sum(heads_out * heads_out, axis=1, keepdims=True) * (1.0 / W)
            normed = heads_out / jnp.sqrt(mean + 1e-5)
            gated_ref[:, :, h * W : (h + 1) * W] = (
                (normed * act_ref[:, h * W : (h + 1) * W]).astype(BF16).reshape(2 * RING, 16, W)
            )

    def run_project():
        w_copy.wait()
        block = [lax.rem(y + i, RING) * 2 for i in range(RING)]
        rows = jnp.concatenate(
            [gated_ref[b + 1 - core] for b in block] + [gated_ref[b + core] for b in block], axis=0
        )

        def project(c):
            columns = pl.ds(pl.multiple_of(c * width, width), width)
            part = jnp.dot(rows, w_ref[:, columns], preferred_element_type=F32)
            pair_out[c] = part[:64].reshape(RING, 16, width)
            pair_copy(c).start()
            own_ref[c] = part[64:].reshape(RING, 16, width)

        each_chunk(project)

    def run_ring():
        def begin(c):
            pair_copy(c).wait_recv()
            own_ref[c] = own_ref[c] + pair_in[c]
            relay_copy(c).start()
            side_copy(c).start()

        def forward(c):
            relay_copy(c).wait_recv()
            block = 1 + 2 * (c // (CHUNKS // 2))
            own_ref[c, block] = own_ref[c, block] + relay_in[c]
            onward_copy(c).start()

        def finish(c):
            side_copy(c).wait_recv()
            onward_copy(c).wait_recv()
            columns = pl.ds(pl.multiple_of(c * width, width), width)
            out_ref[:, columns] = (own_ref[c, 0] + side_in[0, c] + side_in[1, c]).astype(BF16)

        each_chunk(begin)
        each_chunk(forward)
        each_chunk(finish)

    def end_ring():
        def sent(c):
            pair_copy(c).wait_send()
            relay_copy(c).wait_send()
            side_copy(c).wait_send()
            onward_copy(c).wait_send()

        each_chunk(sent)

    phases = (
        (run_maps, end_maps),
        (run_reads, None),
        (run_weights, None),
        (run_gather, None),
        (run_compose, None),
        (run_lines, end_lines),
        (run_starts, end_starts),
        (run_gated, None),
        (run_project, None),
        (run_ring, end_ring),
    )
    for run, end in phases:
        run()
    for run, end in phases:
        if end is not None:
            end()


def on_device(queries, key_vecs, values, out_gate, beta_rates, log_decay, norm_gain, w_out):
    inner, outer = w_out.shape
    width = outer // CHUNKS
    vmem = pl.BlockSpec(memory_space=pltpu.VMEM)
    hbm = pl.BlockSpec(memory_space=pl.ANY)
    dma = pltpu.SemaphoreType.DMA
    square = (W, W)
    return pl.pallas_call(
        layer_kernel,
        name="layer",
        out_shape=jax.ShapeDtypeStruct((16, outer), BF16),
        in_specs=[hbm] * 4 + [vmem] * 3 + [hbm],
        out_specs=vmem,
        scratch_shapes=[
            pltpu.VMEM((W, inner), BF16),
            pltpu.VMEM((STEPS, W, inner), BF16),
            pltpu.VMEM((STEPS, W, inner), BF16),
            pltpu.VMEM((W, inner), BF16),
            pltpu.VMEM((inner, outer), BF16),
            pltpu.VMEM((MICRO, inner), BF16),
            pltpu.VMEM((HEADS, 2) + square, F32),
            pltpu.VMEM((HEADS, 2 * MICRO, 4 * W), BF16),
            pltpu.VMEM((HEADS,) + square, F32),
            pltpu.VMEM((HEADS, W, 2 * W), BF16),
            pltpu.VMEM((W, inner), F32),
            pltpu.VMEM((LINE, 2) + square, F32),
            pltpu.VMEM((LINE * W, 2 * W), BF16),
            pltpu.VMEM((LINE,) + square, F32),
            pltpu.VMEM((2,) + square, F32),
            pltpu.VMEM((2, 2) + square, F32),
            pltpu.VMEM(square, F32),
            pltpu.VMEM((LINE,) + square, F32),
            pltpu.VMEM((HEADS,) + square, F32),
            pltpu.VMEM((2 * RING, 16, inner), BF16),
            pltpu.VMEM((CHUNKS, RING, 16, width), F32),
            pltpu.VMEM((CHUNKS, RING, 16, width), F32),
            pltpu.VMEM((CHUNKS, RING, 16, width), F32),
            pltpu.VMEM((CHUNKS, 16, width), F32),
            pltpu.VMEM((2, CHUNKS, 16, width), F32),
            dma((4,)),
            dma,
            dma((HEADS,)),
            dma((LINE,)),
            dma((3,)),
            dma((3,)),
            dma((LINE,)),
            dma((HEADS,)),
            dma((CHUNKS,)),
            dma((CHUNKS,)),
            dma((3, CHUNKS)),
            dma((3, CHUNKS)),
        ],
        compiler_params=pltpu.CompilerParams(
            collective_id=0, has_side_effects=True, vmem_limit_bytes=56 * 1024 * 1024
        ),
    )(
        queries,
        key_vecs.transpose(1, 0, 2),
        values.transpose(1, 0, 2),
        out_gate,
        beta_rates,
        log_decay,
        norm_gain.reshape(1, W),
        w_out,
    )


def solution(mesh):
    placed = (
        P("seq", "head"),
        P("seq", None, "head"),
        P("seq", None, "head"),
        P("seq", "head"),
        P(None, "head", "seq"),
        P("head", "seq"),
        P(),
        P("head", None),
    )
    return jax.shard_map(
        on_device, mesh=mesh, in_specs=placed, out_specs=P(("seq", "head"), None), check_vma=False
    )
```

```python
import functools

import jax
import jax.numpy as jnp
from jax import lax
from jax.experimental import pallas as pl
from jax.experimental.pallas import tpu as pltpu
from jax.sharding import PartitionSpec as P

F32 = jnp.float32
BF16 = jnp.bfloat16
W = 128
STEPS = 3
MICRO = STEPS * W
HEADS = 4
GROUP = 4
BASE = 16
LINE = 8
ROWS = 4
RING = 4
CHUNKS = 4
MESH = pl.DeviceIdType.MESH


def iota(shape, dim):
    return lax.broadcasted_iota(jnp.int32, shape, dim)


def split(a):
    hi = a.astype(BF16)
    return hi, (a - hi.astype(F32)).astype(BF16)


def split3(a):
    hi, rest = a.astype(BF16), a - a.astype(BF16).astype(F32)
    return (hi,) + split(rest)


def lhs_of(a):
    return jnp.concatenate(split(a), axis=1)


def rhs_of(b):
    pair = jnp.concatenate(split(b), axis=1)
    return jnp.concatenate([pair, pair], axis=0)


def mm(left, right):
    out = jnp.dot(left, right, preferred_element_type=F32)
    half = out.shape[1] // 2
    return out[:, :half] + out[:, half:]


def mm_few(left, right):
    out = jnp.dot(left, right, preferred_element_type=F32)
    rows, columns = out.shape[0] // 2, out.shape[1] // 2
    out = out[:rows] + out[rows:]
    return out[:, :columns] + out[:, columns:]


def nt(a, b):
    return lax.dot_general(a, b, (((1,), (1,)), ((), ())), preferred_element_type=F32)


def local_maps(raw_ref, v_ref, beta_ref, decay_ref, k_ref, tf_ref, x_ref, v_wait):
    time_i, flat_i = iota((MICRO, MICRO), 0), iota((MICRO, MICRO), 1)
    to_time = (STEPS * lax.rem(flat_i, W) + flat_i // W == time_i).astype(BF16)
    raw = raw_ref[...].reshape(MICRO, HEADS * W)
    k_ref[...] = jnp.dot(to_time, raw, preferred_element_type=F32).astype(BF16)
    upto = (STEPS * iota((MICRO, W), 1) <= iota((MICRO, W), 0)).astype(BF16)
    upto = jnp.concatenate([upto] * 3, axis=1)
    decay = jnp.concatenate(split3(jnp.maximum(decay_ref[...], -110.0)), axis=1)
    g_col = nt(upto, decay)
    g_row = nt(decay, upto)
    beta = jnp.concatenate([beta_ref[j] for j in range(STEPS)], axis=1)
    b_col = nt(jnp.concatenate([to_time] * 3, axis=1), jnp.concatenate(split3(beta), axis=1))
    row_i, col_i = iota((W, W), 0), iota((W, W), 1)
    strict = row_i > col_i
    eye = (row_i == col_i).astype(F32)
    ones = jnp.ones((8, 2 * W), BF16)
    lane_block = iota((BASE, W), 1) // BASE
    r_cols, r_rows, systems, packed = [], [], [], []
    for h in range(HEADS):
        keys = k_ref[:, h * W : (h + 1) * W]
        wide = keys.astype(F32)
        squares = wide * wide
        r_c = 1.0 / jnp.sqrt(jnp.sum(squares, axis=1, keepdims=True) + 1e-6)
        r_r = 1.0 / jnp.sqrt(nt(ones, lhs_of(squares))[0:1] + 1e-6)
        r_cols.append(r_c)
        r_rows.append(r_r)
        scale = b_col[:, h : h + 1] * r_c
        blocks = {}
        for i in range(3):
            for j in range(i + 1):
                si, sj = slice(i * W, (i + 1) * W), slice(j * W, (j + 1) * W)
                gap = g_col[si, h : h + 1] - g_row[h : h + 1, sj]
                if i == j:
                    gap = jnp.where(strict, gap, 0.0)
                a = nt(keys[si], keys[sj]) * (scale[si] * r_r[:, sj]) * jnp.exp(gap)
                if i == j:
                    a = jnp.where(strict, a, 0.0)
                    packed.append(
                        sum(
                            jnp.where(lane_block == b, a[b * BASE : (b + 1) * BASE], 0.0)
                            for b in range(W // BASE)
                        )
                    )
                blocks[i, j] = a
        systems.append(blocks)
    count = len(packed)
    packed = lhs_of(jnp.concatenate(packed, axis=0))
    block_start = (col_i // BASE) * BASE
    small = [
        (iota((count, 8, W), 1) + 8 * s == iota((count, 8, W), 2) % BASE).astype(F32)
        for s in range(BASE // 8)
    ]
    for j in range(BASE - 1):
        pick = (row_i == block_start + j).astype(BF16)
        factor = jnp.dot(
            packed, jnp.concatenate([pick, pick], axis=0), preferred_element_type=F32
        ).reshape(count, BASE, W)
        first = j // 8
        row = small[first][:, j % 8 : j % 8 + 1, :]
        for s in range(first, BASE // 8):
            small[s] = small[s] - factor[:, 8 * s : 8 * s + 8, :] * row
    row_p, col_p = iota((W, 2 * W), 0), lax.rem(iota((W, 2 * W), 1), W)
    widths = [n for n in (16, 32, 64) if n >= BASE]
    same = {n: (row_p // n == col_p // n).astype(F32) for n in widths + [W]}
    low = {n: (same[2 * n] - same[n]).astype(BF16) for n in widths}
    same = {n: same[n].astype(BF16) for n in widths}
    for group in range(0, HEADS, GROUP):
        heads = range(group, group + GROUP)
        inverse = {
            (h, i): jnp.concatenate([small[s][h * 3 + i] for s in range(BASE // 8)], axis=0)
            for h in heads
            for i in range(3)
        }
        below = {n: lhs_of(systems[n[0]][n[1], n[1]]) for n in inverse}
        for width in widths:
            even = lax.rem(iota((width, W), 1) // width, 2) == 0
            left = {n: split(inv) for n, inv in inverse.items()}
            step = {}
            for n in inverse:
                rows = jnp.concatenate(left[n], axis=0)
                step[n] = mm_few(rows, below[n] * low[width])
            for n, inv in inverse.items():
                full = jnp.concatenate([jnp.concatenate(left[n], axis=1)] * (W // width), axis=0)
                rows = jnp.concatenate(split(step[n]), axis=0)
                corner = mm_few(rows, full * same[width])
                inverse[n] = jnp.concatenate(
                    [jnp.where(even, inv, 0.0), jnp.where(even, -corner, inv)], axis=0
                )
        v_wait()
        wide, right, x1, x1r, x2, x3, solved = {}, {}, {}, {}, {}, {}, {}
        values = v_ref[...].reshape(MICRO, HEADS * W)
        values = jnp.dot(to_time, values, preferred_element_type=F32)
        for h in heads:
            b_c, g_c = b_col[:, h : h + 1], g_col[:, h : h + 1]
            wide[h] = k_ref[:, h * W : (h + 1) * W].astype(F32)
            right[h] = jnp.concatenate(
                [
                    b_c * values[:, h * W : (h + 1) * W],
                    (b_c * jnp.exp(g_c) * r_cols[h]) * wide[h],
                ],
                axis=1,
            )
        for h in heads:
            x1[h] = mm(lhs_of(inverse[h, 0]), rhs_of(right[h][:W]))
        for h in heads:
            x1r[h] = rhs_of(x1[h])
            x2[h] = right[h][W : 2 * W] - mm(lhs_of(systems[h][1, 0]), x1r[h])
        for h in heads:
            x2[h] = mm(lhs_of(inverse[h, 1]), rhs_of(x2[h]))
        for h in heads:
            x3[h] = right[h][2 * W :] - mm(lhs_of(systems[h][2, 0]), x1r[h])
        for h in heads:
            x3[h] = x3[h] - mm(lhs_of(systems[h][2, 1]), rhs_of(x2[h]))
        for h in heads:
            x3[h] = mm(lhs_of(inverse[h, 2]), rhs_of(x3[h]))
        for h in heads:
            solved = jnp.concatenate([x1[h], x2[h], x3[h]], axis=0)
            x_ref[h] = solved
            g_c, g_end = g_col[:, h : h + 1], g_col[MICRO - 1 : MICRO, h : h + 1]
            tail = jnp.concatenate(split((r_cols[h] * jnp.exp(g_end - g_c)) * solved), axis=1)
            out = jnp.dot(wide[h].T.astype(BF16), tail, preferred_element_type=F32)
            out = out[:, : 2 * W] + out[:, 2 * W :]
            tf_ref[h, 0] = jnp.exp(g_end) * eye - out[:, W:]
            tf_ref[h, 1] = out[:, :W]
    return g_row, r_rows


def local_reads(q_ref, k_ref, decay_ref, x_ref, g_row, r_rows, lo_ref, lq_ref):
    decay = jnp.concatenate(split3(jnp.maximum(decay_ref[...], -110.0)), axis=1)
    upto = (iota((W, W), 1) <= iota((W, W), 0)).astype(BF16)
    q_col = nt(jnp.concatenate([upto] * 3, axis=1), decay)
    visible = iota((W, MICRO), 1) <= STEPS * iota((W, MICRO), 0) + STEPS - 1
    heads = range(HEADS)
    query = [q_ref[:, h * W : (h + 1) * W] for h in heads]
    scores = [nt(query[h], k_ref[:, h * W : (h + 1) * W]) for h in heads]
    gaps = [jnp.where(visible, q_col[:, h : h + 1] - g_row[h : h + 1, :], 0.0) for h in heads]
    scores = [jnp.where(visible, scores[h] * (r_rows[h] * jnp.exp(gaps[h])), 0.0) for h in heads]
    reads = [mm(lhs_of(scores[h]), rhs_of(x_ref[h])) for h in heads]
    for h in heads:
        lo_ref[h] = reads[h][:, :W]
        lq_ref[h] = lhs_of(jnp.exp(q_col[:, h : h + 1]) * query[h].astype(F32) - reads[h][:, W:])


def compose(lefts, right):
    out = mm(
        jnp.concatenate([lhs_of(t) for t, f in lefts], axis=0),
        rhs_of(jnp.concatenate(right, axis=1)),
    )
    return [
        (out[i * W : (i + 1) * W, :W], out[i * W : (i + 1) * W, W:] + lefts[i][1])
        for i in range(len(lefts))
    ]


def layer_kernel(
    q_hbm, k_hbm, v_hbm, gate_hbm, beta_ref, decay_ref, gain_ref, w_hbm, out_ref,
    q_ref, raw_ref, v_ref, gate_ref, w_ref, keys_ref, tf_ref, x_ref, lo_ref, lq_ref, act_ref,
    maps_ref, pre_t_ref, pre_f_ref, total_ref, far_ref, line_ref, given_ref, start_ref,
    gated_ref, pair_out, pair_in, own_ref, relay_in, side_in,
    in_sem, w_sem, map_send, map_recv, line_send, line_recv, start_send, start_recv,
    pair_send, pair_recv, ring_send, ring_recv,
):
    seq, head = lax.axis_index("seq"), lax.axis_index("head")
    x, z = seq // LINE, lax.rem(seq, LINE)
    y, core = head // 2, lax.rem(head, 2)
    line = x * LINE
    owner = core == 1
    mine, mine_core = z // 2, lax.rem(z, 2)
    width = w_ref.shape[1] // CHUNKS
    held = {}

    def at(s, h):
        return {"device_id": (s, h), "device_id_type": MESH}

    owners, served = y * 2 + 1, y * 2 + mine_core
    up = lax.rem(y + 1, RING) * 2 + core
    down = lax.rem(y + RING - 1, RING) * 2 + core
    sibling = y * 2 + 1 - core

    inputs = ((k_hbm, raw_ref), (v_hbm, v_ref), (q_hbm, q_ref), (gate_hbm, gate_ref))

    def in_copy(i):
        return pltpu.make_async_copy(*inputs[i], in_sem.at[i])

    for i in range(4):
        in_copy(i).start()
    w_copy = pltpu.make_async_copy(w_hbm, w_ref, w_sem)

    barrier = pltpu.get_barrier_semaphore()
    for i in range(1, LINE):
        for h in (head, sibling):
            pl.semaphore_signal(barrier, inc=1, **at(line + lax.rem(z + i, LINE), h))
    for i in range(1, ROWS):
        pl.semaphore_signal(barrier, inc=1, **at(lax.rem(x + i, ROWS) * LINE + z, head))
    for h in (up, down, sibling):
        pl.semaphore_signal(barrier, inc=1, **at(seq, h))

    def map_copy(h):
        return pltpu.make_async_remote_copy(
            src_ref=tf_ref.at[h], dst_ref=maps_ref.at[z],
            send_sem=map_send.at[h], recv_sem=map_recv.at[z],
            **at(line + 2 * h + core, owners),
        )

    def line_copy(src, dst, send, recv, to):
        return pltpu.make_async_remote_copy(
            src_ref=src, dst_ref=dst, send_sem=line_send.at[send], recv_sem=line_recv.at[recv],
            **at(to * LINE + z, head),
        )

    def start_copy(to, h):
        return pltpu.make_async_remote_copy(
            src_ref=given_ref.at[to], dst_ref=start_ref.at[h],
            send_sem=start_send.at[to], recv_sem=start_recv.at[h], **at(line + to, served),
        )

    def pair_copy(c):
        return pltpu.make_async_remote_copy(
            src_ref=pair_out.at[c], dst_ref=pair_in.at[c],
            send_sem=pair_send.at[c], recv_sem=pair_recv.at[c], **at(seq, sibling),
        )

    def ring_copy(kind, c, src, dst, upward):
        return pltpu.make_async_remote_copy(
            src_ref=src, dst_ref=dst, send_sem=ring_send.at[kind, c], recv_sem=ring_recv.at[kind, c],
            **at(seq, jnp.where(upward, up, down)),
        )

    def relay_copy(c):
        return ring_copy(0, c, own_ref.at[c, 2], relay_in.at[c], c < CHUNKS // 2)

    def side_copy(c):
        part = c // (CHUNKS // 2)
        return ring_copy(1, c, own_ref.at[c, 3 - 2 * part], side_in.at[1 - part, c], part == 1)

    def onward_copy(c):
        part = c // (CHUNKS // 2)
        return ring_copy(2, c, own_ref.at[c, 1 + 2 * part], side_in.at[part, c], part == 0)

    def each_chunk(body):
        def step(i, carry):
            body(lax.rem(i, 2) * (CHUNKS // 2) + i // 2)
            return carry

        lax.fori_loop(0, CHUNKS, step, 0)

    def run_maps():
        in_copy(0).wait()
        held["rows"] = local_maps(
            raw_ref, v_ref, beta_ref, decay_ref, keys_ref, tf_ref, x_ref, in_copy(1).wait
        )
        pl.semaphore_wait(barrier, 2 * (LINE - 1) + ROWS - 1 + 3)
        for h in (1, 0, 2, 3):
            keep = owner & (z == 2 * h + 1)

            @pl.when(jnp.logical_not(keep))
            def _():
                map_copy(h).start()

            @pl.when(keep)
            def _():
                maps_ref[z] = tf_ref[h]

    def end_maps():
        for h in range(HEADS):
            @pl.when(jnp.logical_not(owner & (z == 2 * h + 1)))
            def _():
                map_copy(h).wait_send()

    def run_reads():
        g_row, r_rows = held["rows"]
        in_copy(2).wait()
        in_copy(3).wait()
        local_reads(q_ref, keys_ref, decay_ref, x_ref, g_row, r_rows, lo_ref, lq_ref)
        gate = gate_ref[...].astype(F32)
        act_ref[...] = (gate / (1.0 + jnp.exp(-gate))) * jnp.concatenate(
            [gain_ref[...]] * HEADS, axis=1
        )

    def run_gather():
        @pl.when(owner)
        def _():
            def arrived(other):
                pltpu.make_async_remote_copy(
                    src_ref=tf_ref.at[0], dst_ref=maps_ref.at[other],
                    send_sem=map_send.at[0], recv_sem=map_recv.at[other], **at(line + other, sibling),
                ).wait_recv()

            for i in range(1, LINE):
                arrived(lax.rem(z + i, LINE))

            @pl.when(mine_core == 0)
            def _():
                arrived(z)

    def run_compose():
        @pl.when(owner)
        def _():
            m = [(maps_ref[i, 0], maps_ref[i, 1]) for i in range(LINE)]
            (p1,) = compose([m[1]], m[0])
            (q23,) = compose([m[3]], m[2])
            (q45,) = compose([m[5]], m[4])
            (q67,) = compose([m[7]], m[6])
            p2, p3 = compose([m[2], q23], p1)
            q46, q47 = compose([m[6], q67], q45)
            p4, p5, p6, p7 = compose([m[4], q45, q46, q47], p3)
            total_ref[0] = p7[0]
            total_ref[1] = p7[1]
            for i, (t, f) in enumerate((m[0], p1, p2, p3, p4, p5, p6, p7)):
                pre_t_ref[i * W : (i + 1) * W] = lhs_of(t)
                pre_f_ref[i] = f

    def run_weights():
        w_copy.start()

    def run_lines():
        @pl.when(owner)
        def _():
            @pl.when(x == 0)
            def _():
                for i, to in enumerate((3, 1, 2)):
                    line_copy(total_ref.at[1], line_ref, i, 0, to).start()
                given_ref[0] = jnp.zeros((W, W), F32)

            @pl.when(x == 1)
            def _():
                for i, to in enumerate((3, 2)):
                    line_copy(total_ref, far_ref.at[0], i, 1, to).start()

            @pl.when(x == 2)
            def _():
                line_copy(total_ref, far_ref.at[1], 0, 2, 3).start()

            @pl.when(x > 0)
            def _():
                line_copy(total_ref.at[1], line_ref, 0, 0, 1).wait_recv()
                given_ref[0] = line_ref[...]

            @pl.when(x > 1)
            def _():
                begin = rhs_of(line_ref[...])
                line_copy(total_ref, far_ref.at[0], 0, 1, 3).wait_recv()
                given_ref[0] = mm(lhs_of(far_ref[0, 0]), begin) + far_ref[0, 1]

            @pl.when(x == 3)
            def _():
                line_copy(total_ref, far_ref.at[1], 0, 2, 3).wait_recv()
                given_ref[0] = mm(lhs_of(far_ref[1, 0]), rhs_of(given_ref[0])) + far_ref[1, 1]

    def end_lines():
        @pl.when(owner)
        def _():
            @pl.when(x == 0)
            def _():
                for i, to in enumerate((3, 1, 2)):
                    line_copy(total_ref.at[1], line_ref, i, 0, to).wait_send()

            @pl.when(x == 1)
            def _():
                for i, to in enumerate((3, 2)):
                    line_copy(total_ref, far_ref.at[0], i, 1, to).wait_send()

            @pl.when(x == 2)
            def _():
                line_copy(total_ref, far_ref.at[1], 0, 2, 3).wait_send()

    def run_starts():
        def give(to):
            keep = (z == to) & (mine_core == 1)

            @pl.when(jnp.logical_not(keep))
            def _():
                start_copy(to, mine).start()

            @pl.when(keep)
            def _():
                start_ref[mine] = given_ref[to]

        @pl.when(owner)
        def _():
            give(0)
            for batch in ((1, 2, 3, 7), (4, 5, 6)):
                @pl.when(x == 0)
                def _():
                    for to in batch:
                        given_ref[to] = pre_f_ref[to - 1]

                @pl.when(x > 0)
                def _():
                    begin = rhs_of(given_ref[0])
                    after = [mm(pre_t_ref[(to - 1) * W : to * W], begin) for to in batch]
                    for to, part in zip(batch, after):
                        given_ref[to] = part + pre_f_ref[to - 1]

                for to in batch:
                    give(to)

        for h in range(HEADS):
            @pl.when(jnp.logical_not(owner & (z == 2 * h + 1)))
            def _():
                start_copy(0, h).wait_recv()

    def end_starts():
        @pl.when(owner)
        def _():
            for to in range(LINE):
                @pl.when(jnp.logical_not((z == to) & (mine_core == 1)))
                def _():
                    start_copy(to, mine).wait_send()

    def run_gated():
        for h in range(HEADS):
            heads_out = lo_ref[h] + mm(lq_ref[h], rhs_of(start_ref[h]))
            mean = jnp.sum(heads_out * heads_out, axis=1, keepdims=True) * (1.0 / W)
            normed = heads_out / jnp.sqrt(mean + 1e-5)
            gated_ref[:, :, h * W : (h + 1) * W] = (
                (normed * act_ref[:, h * W : (h + 1) * W]).astype(BF16).reshape(2 * RING, 16, W)
            )

    def run_project():
        w_copy.wait()
        block = [lax.rem(y + i, RING) * 2 for i in range(RING)]
        rows = jnp.concatenate(
            [gated_ref[b + 1 - core] for b in block] + [gated_ref[b + core] for b in block], axis=0
        )

        def project(c):
            columns = pl.ds(pl.multiple_of(c * width, width), width)
            part = jnp.dot(rows, w_ref[:, columns], preferred_element_type=F32)
            pair_out[c] = part[:64].reshape(RING, 16, width)
            pair_copy(c).start()
            own_ref[c] = part[64:].reshape(RING, 16, width)

        each_chunk(project)

    def run_ring():
        def begin(c):
            pair_copy(c).wait_recv()
            own_ref[c] = own_ref[c] + pair_in[c]
            relay_copy(c).start()
            side_copy(c).start()

        def forward(c):
            relay_copy(c).wait_recv()
            block = 1 + 2 * (c // (CHUNKS // 2))
            own_ref[c, block] = own_ref[c, block] + relay_in[c]
            onward_copy(c).start()

        def finish(c):
            side_copy(c).wait_recv()
            onward_copy(c).wait_recv()
            columns = pl.ds(pl.multiple_of(c * width, width), width)
            out_ref[:, columns] = (own_ref[c, 0] + side_in[0, c] + side_in[1, c]).astype(BF16)

        each_chunk(begin)
        each_chunk(forward)
        each_chunk(finish)

    def end_ring():
        def sent(c):
            pair_copy(c).wait_send()
            relay_copy(c).wait_send()
            side_copy(c).wait_send()
            onward_copy(c).wait_send()

        each_chunk(sent)

    phases = (
        (run_maps, end_maps),
        (run_reads, None),
        (run_weights, None),
        (run_gather, None),
        (run_compose, None),
        (run_lines, end_lines),
        (run_starts, end_starts),
        (run_gated, None),
        (run_project, None),
        (run_ring, end_ring),
    )
    for run, end in phases:
        run()
    for run, end in phases:
        if end is not None:
            end()


def on_device(queries, key_vecs, values, out_gate, beta_rates, log_decay, norm_gain, w_out):
    inner, outer = w_out.shape
    width = outer // CHUNKS
    vmem = pl.BlockSpec(memory_space=pltpu.VMEM)
    hbm = pl.BlockSpec(memory_space=pl.ANY)
    dma = pltpu.SemaphoreType.DMA
    square = (W, W)
    return pl.pallas_call(
        layer_kernel,
        name="layer",
        out_shape=jax.ShapeDtypeStruct((16, outer), BF16),
        in_specs=[hbm] * 4 + [vmem] * 3 + [hbm],
        out_specs=vmem,
        scratch_shapes=[
            pltpu.VMEM((W, inner), BF16),
            pltpu.VMEM((STEPS, W, inner), BF16),
            pltpu.VMEM((STEPS, W, inner), BF16),
            pltpu.VMEM((W, inner), BF16),
            pltpu.VMEM((inner, outer), BF16),
            pltpu.VMEM((MICRO, inner), BF16),
            pltpu.VMEM((HEADS, 2) + square, F32),
            pltpu.VMEM((HEADS, MICRO, 2 * W), F32),
            pltpu.VMEM((HEADS,) + square, F32),
            pltpu.VMEM((HEADS, W, 2 * W), BF16),
            pltpu.VMEM((W, inner), F32),
            pltpu.VMEM((LINE, 2) + square, F32),
            pltpu.VMEM((LINE * W, 2 * W), BF16),
            pltpu.VMEM((LINE,) + square, F32),
            pltpu.VMEM((2,) + square, F32),
            pltpu.VMEM((2, 2) + square, F32),
            pltpu.VMEM(square, F32),
            pltpu.VMEM((LINE,) + square, F32),
            pltpu.VMEM((HEADS,) + square, F32),
            pltpu.VMEM((2 * RING, 16, inner), BF16),
            pltpu.VMEM((CHUNKS, RING, 16, width), F32),
            pltpu.VMEM((CHUNKS, RING, 16, width), F32),
            pltpu.VMEM((CHUNKS, RING, 16, width), F32),
            pltpu.VMEM((CHUNKS, 16, width), F32),
            pltpu.VMEM((2, CHUNKS, 16, width), F32),
            dma((4,)),
            dma,
            dma((HEADS,)),
            dma((LINE,)),
            dma((3,)),
            dma((3,)),
            dma((LINE,)),
            dma((HEADS,)),
            dma((CHUNKS,)),
            dma((CHUNKS,)),
            dma((3, CHUNKS)),
            dma((3, CHUNKS)),
        ],
        compiler_params=pltpu.CompilerParams(
            collective_id=0, has_side_effects=True, vmem_limit_bytes=56 * 1024 * 1024
        ),
    )(
        queries,
        key_vecs.transpose(1, 0, 2),
        values.transpose(1, 0, 2),
        out_gate,
        beta_rates,
        log_decay,
        norm_gain.reshape(1, W),
        w_out,
    )


def solution(mesh):
    placed = (
        P("seq", "head"),
        P("seq", None, "head"),
        P("seq", None, "head"),
        P("seq", "head"),
        P(None, "head", "seq"),
        P("head", "seq"),
        P(),
        P("head", None),
    )
    return jax.shard_map(
        on_device, mesh=mesh, in_specs=placed, out_specs=P(("seq", "head"), None), check_vma=False
    )
```

```python
import functools

import jax
import jax.numpy as jnp
from jax import lax
from jax.experimental import pallas as pl
from jax.experimental.pallas import tpu as pltpu
from jax.sharding import PartitionSpec as P

F32 = jnp.float32
BF16 = jnp.bfloat16
W = 128
STEPS = 3
MICRO = STEPS * W
HEADS = 4
GROUP = 4
BASE = 16
LINE = 8
ROWS = 4
RING = 4
CHUNKS = 4
MESH = pl.DeviceIdType.MESH


def iota(shape, dim):
    return lax.broadcasted_iota(jnp.int32, shape, dim)


def split(a):
    hi = a.astype(BF16)
    return hi, (a - hi.astype(F32)).astype(BF16)


def split3(a):
    hi, rest = a.astype(BF16), a - a.astype(BF16).astype(F32)
    return (hi,) + split(rest)


def lhs_of(a):
    return jnp.concatenate(split(a), axis=1)


def rhs_of(b):
    pair = jnp.concatenate(split(b), axis=1)
    return jnp.concatenate([pair, pair], axis=0)


def mm(left, right):
    out = jnp.dot(left, right, preferred_element_type=F32)
    half = out.shape[1] // 2
    return out[:, :half] + out[:, half:]


def mm_few(left, right):
    out = jnp.dot(left, right, preferred_element_type=F32)
    rows, columns = out.shape[0] // 2, out.shape[1] // 2
    out = out[:rows] + out[rows:]
    return out[:, :columns] + out[:, columns:]


def nt(a, b):
    return lax.dot_general(a, b, (((1,), (1,)), ((), ())), preferred_element_type=F32)


def local_maps(raw_ref, v_ref, beta_ref, decay_ref, k_ref, tf_ref, x_ref, v_wait):
    time_i, flat_i = iota((MICRO, MICRO), 0), iota((MICRO, MICRO), 1)
    to_time = (STEPS * lax.rem(flat_i, W) + flat_i // W == time_i).astype(BF16)
    raw = raw_ref[...].reshape(MICRO, HEADS * W)
    k_ref[...] = jnp.dot(to_time, raw, preferred_element_type=F32).astype(BF16)
    upto = (STEPS * iota((MICRO, W), 1) <= iota((MICRO, W), 0)).astype(BF16)
    upto = jnp.concatenate([upto] * 3, axis=1)
    decay = jnp.concatenate(split3(jnp.maximum(decay_ref[...], -110.0)), axis=1)
    g_col = nt(upto, decay)
    g_row = nt(decay, upto)
    beta = jnp.concatenate([beta_ref[j] for j in range(STEPS)], axis=1)
    b_col = nt(jnp.concatenate([to_time] * 3, axis=1), jnp.concatenate(split3(beta), axis=1))
    row_i, col_i = iota((W, W), 0), iota((W, W), 1)
    strict = row_i > col_i
    eye = (row_i == col_i).astype(F32)
    ones = jnp.ones((8, 2 * W), BF16)
    lane_block = iota((BASE, W), 1) // BASE
    r_cols, r_rows, systems, packed = [], [], [], []
    for h in range(HEADS):
        keys = k_ref[:, h * W : (h + 1) * W]
        wide = keys.astype(F32)
        squares = wide * wide
        r_c = 1.0 / jnp.sqrt(jnp.sum(squares, axis=1, keepdims=True) + 1e-6)
        r_r = 1.0 / jnp.sqrt(nt(ones, lhs_of(squares))[0:1] + 1e-6)
        r_cols.append(r_c)
        r_rows.append(r_r)
        scale = b_col[:, h : h + 1] * r_c
        blocks = {}
        for i in range(3):
            for j in range(i + 1):
                si, sj = slice(i * W, (i + 1) * W), slice(j * W, (j + 1) * W)
                gap = g_col[si, h : h + 1] - g_row[h : h + 1, sj]
                if i == j:
                    gap = jnp.where(strict, gap, 0.0)
                a = nt(keys[si], keys[sj]) * (scale[si] * r_r[:, sj]) * jnp.exp(gap)
                if i == j:
                    a = jnp.where(strict, a, 0.0)
                    packed.append(
                        sum(
                            jnp.where(lane_block == b, a[b * BASE : (b + 1) * BASE], 0.0)
                            for b in range(W // BASE)
                        )
                    )
                blocks[i, j] = a
        systems.append(blocks)
    count = len(packed)
    packed = lhs_of(jnp.concatenate(packed, axis=0))
    block_start = (col_i // BASE) * BASE
    small = [
        (iota((count, 8, W), 1) + 8 * s == iota((count, 8, W), 2) % BASE).astype(F32)
        for s in range(BASE // 8)
    ]
    for j in range(BASE - 1):
        pick = (row_i == block_start + j).astype(BF16)
        factor = jnp.dot(
            packed, jnp.concatenate([pick, pick], axis=0), preferred_element_type=F32
        ).reshape(count, BASE, W)
        first = j // 8
        row = small[first][:, j % 8 : j % 8 + 1, :]
        for s in range(first, BASE // 8):
            small[s] = small[s] - factor[:, 8 * s : 8 * s + 8, :] * row
    row_p, col_p = iota((W, 2 * W), 0), lax.rem(iota((W, 2 * W), 1), W)
    widths = [n for n in (16, 32, 64) if n >= BASE]
    same = {n: (row_p // n == col_p // n).astype(F32) for n in widths + [W]}
    low = {n: (same[2 * n] - same[n]).astype(BF16) for n in widths}
    same = {n: same[n].astype(BF16) for n in widths}
    for group in range(0, HEADS, GROUP):
        heads = range(group, group + GROUP)
        inverse = {
            (h, i): jnp.concatenate([small[s][h * 3 + i] for s in range(BASE // 8)], axis=0)
            for h in heads
            for i in range(3)
        }
        below = {n: lhs_of(systems[n[0]][n[1], n[1]]) for n in inverse}
        for width in widths:
            even = lax.rem(iota((width, W), 1) // width, 2) == 0
            left = {n: split(inv) for n, inv in inverse.items()}
            step = {}
            for n in inverse:
                rows = jnp.concatenate(left[n], axis=0)
                step[n] = mm_few(rows, below[n] * low[width])
            for n, inv in inverse.items():
                full = jnp.concatenate([jnp.concatenate(left[n], axis=1)] * (W // width), axis=0)
                rows = jnp.concatenate(split(step[n]), axis=0)
                corner = mm_few(rows, full * same[width])
                inverse[n] = jnp.concatenate(
                    [jnp.where(even, inv, 0.0), jnp.where(even, -corner, inv)], axis=0
                )
        v_wait()
        wide, right, x1, x1r, x2, x3, solved = {}, {}, {}, {}, {}, {}, {}
        values = v_ref[...].reshape(MICRO, HEADS * W)
        values = jnp.dot(to_time, values, preferred_element_type=F32)
        for h in heads:
            b_c, g_c = b_col[:, h : h + 1], g_col[:, h : h + 1]
            wide[h] = k_ref[:, h * W : (h + 1) * W].astype(F32)
            right[h] = jnp.concatenate(
                [
                    b_c * values[:, h * W : (h + 1) * W],
                    (b_c * jnp.exp(g_c) * r_cols[h]) * wide[h],
                ],
                axis=1,
            )
        for h in heads:
            x1[h] = mm(lhs_of(inverse[h, 0]), rhs_of(right[h][:W]))
        for h in heads:
            x1r[h] = rhs_of(x1[h])
            x2[h] = right[h][W : 2 * W] - mm(lhs_of(systems[h][1, 0]), x1r[h])
        for h in heads:
            x2[h] = mm(lhs_of(inverse[h, 1]), rhs_of(x2[h]))
        for h in heads:
            x3[h] = right[h][2 * W :] - mm(lhs_of(systems[h][2, 0]), x1r[h])
        for h in heads:
            x3[h] = x3[h] - mm(lhs_of(systems[h][2, 1]), rhs_of(x2[h]))
        for h in heads:
            x3[h] = mm(lhs_of(inverse[h, 2]), rhs_of(x3[h]))
        for h in heads:
            solved = jnp.concatenate([x1[h], x2[h], x3[h]], axis=0)
            x_ref[h] = solved
            g_c, g_end = g_col[:, h : h + 1], g_col[MICRO - 1 : MICRO, h : h + 1]
            tail = jnp.concatenate(split((r_cols[h] * jnp.exp(g_end - g_c)) * solved), axis=1)
            out = jnp.dot(wide[h].T.astype(BF16), tail, preferred_element_type=F32)
            out = out[:, : 2 * W] + out[:, 2 * W :]
            tf_ref[h, 0] = jnp.exp(g_end) * eye - out[:, W:]
            tf_ref[h, 1] = out[:, :W]
    return g_row, r_rows


def local_reads(q_ref, k_ref, decay_ref, x_ref, g_row, r_rows, lo_ref, lq_ref):
    decay = jnp.concatenate(split3(jnp.maximum(decay_ref[...], -110.0)), axis=1)
    upto = (iota((W, W), 1) <= iota((W, W), 0)).astype(BF16)
    q_col = nt(jnp.concatenate([upto] * 3, axis=1), decay)
    visible = iota((W, MICRO), 1) <= STEPS * iota((W, MICRO), 0) + STEPS - 1
    heads = range(HEADS)
    query = [q_ref[:, h * W : (h + 1) * W] for h in heads]
    scores = [nt(query[h], k_ref[:, h * W : (h + 1) * W]) for h in heads]
    gaps = [jnp.where(visible, q_col[:, h : h + 1] - g_row[h : h + 1, :], 0.0) for h in heads]
    scores = [jnp.where(visible, scores[h] * (r_rows[h] * jnp.exp(gaps[h])), 0.0) for h in heads]
    reads = [mm(lhs_of(scores[h]), rhs_of(x_ref[h])) for h in heads]
    for h in heads:
        lo_ref[h] = reads[h][:, :W]
        lq_ref[h] = lhs_of(jnp.exp(q_col[:, h : h + 1]) * query[h].astype(F32) - reads[h][:, W:])


def compose(lefts, right):
    out = mm(
        jnp.concatenate([lhs_of(t) for t, f in lefts], axis=0),
        rhs_of(jnp.concatenate(right, axis=1)),
    )
    return [
        (out[i * W : (i + 1) * W, :W], out[i * W : (i + 1) * W, W:] + lefts[i][1])
        for i in range(len(lefts))
    ]


def layer_kernel(
    q_hbm, k_hbm, v_hbm, gate_hbm, beta_ref, decay_ref, gain_ref, w_hbm, out_ref,
    q_ref, raw_ref, v_ref, gate_ref, w_ref, keys_ref, tf_ref, x_ref, lo_ref, lq_ref, act_ref,
    maps_ref, pre_t_ref, pre_f_ref, total_ref, far_ref, line_ref, given_ref, start_ref,
    gated_ref, pair_out, pair_in, own_ref, relay_in, side_in,
    in_sem, w_sem, map_send, map_recv, line_send, line_recv, start_send, start_recv,
    pair_send, pair_recv, ring_send, ring_recv,
):
    seq, head = lax.axis_index("seq"), lax.axis_index("head")
    x, z = seq // LINE, lax.rem(seq, LINE)
    y, core = head // 2, lax.rem(head, 2)
    line = x * LINE
    owner = core == 1
    mine, mine_core = z // 2, lax.rem(z, 2)
    width = w_ref.shape[1] // CHUNKS
    held = {}

    def at(s, h):
        return {"device_id": (s, h), "device_id_type": MESH}

    owners, served = y * 2 + 1, y * 2 + mine_core
    up = lax.rem(y + 1, RING) * 2 + core
    down = lax.rem(y + RING - 1, RING) * 2 + core
    sibling = y * 2 + 1 - core

    inputs = ((k_hbm, raw_ref), (v_hbm, v_ref), (q_hbm, q_ref), (gate_hbm, gate_ref))

    def in_copy(i):
        return pltpu.make_async_copy(*inputs[i], in_sem.at[i])

    for i in range(4):
        in_copy(i).start()
    w_copy = pltpu.make_async_copy(w_hbm, w_ref, w_sem)

    barrier = pltpu.get_barrier_semaphore()
    for i in range(1, LINE):
        for h in (head, sibling):
            pl.semaphore_signal(barrier, inc=1, **at(line + lax.rem(z + i, LINE), h))
    for i in range(1, ROWS):
        pl.semaphore_signal(barrier, inc=1, **at(lax.rem(x + i, ROWS) * LINE + z, head))
    for h in (up, down, sibling):
        pl.semaphore_signal(barrier, inc=1, **at(seq, h))

    def map_copy(h):
        return pltpu.make_async_remote_copy(
            src_ref=tf_ref.at[h], dst_ref=maps_ref.at[z],
            send_sem=map_send.at[h], recv_sem=map_recv.at[z],
            **at(line + 2 * h + core, owners),
        )

    def line_copy(src, dst, send, recv, to):
        return pltpu.make_async_remote_copy(
            src_ref=src, dst_ref=dst, send_sem=line_send.at[send], recv_sem=line_recv.at[recv],
            **at(to * LINE + z, head),
        )

    def start_copy(to, h):
        return pltpu.make_async_remote_copy(
            src_ref=given_ref.at[to], dst_ref=start_ref.at[h],
            send_sem=start_send.at[to], recv_sem=start_recv.at[h], **at(line + to, served),
        )

    def pair_copy(c, kind):
        part = pl.ds(0, 1) if kind == 0 else pl.ds(1, RING - 1)
        return pltpu.make_async_remote_copy(
            src_ref=pair_out.at[c, part], dst_ref=pair_in.at[c, part],
            send_sem=pair_send.at[kind, c], recv_sem=pair_recv.at[kind, c], **at(seq, sibling),
        )

    def ring_copy(kind, c, src, dst, upward):
        return pltpu.make_async_remote_copy(
            src_ref=src, dst_ref=dst, send_sem=ring_send.at[kind, c], recv_sem=ring_recv.at[kind, c],
            **at(seq, jnp.where(upward, up, down)),
        )

    def relay_copy(c):
        return ring_copy(0, c, own_ref.at[c, 0], relay_in.at[c], c < CHUNKS // 2)

    def side_copy(c):
        part = c // (CHUNKS // 2)
        return ring_copy(1, c, own_ref.at[c, 3 - part], side_in.at[1 - part, c], part == 1)

    def onward_copy(c):
        part = c // (CHUNKS // 2)
        return ring_copy(2, c, own_ref.at[c, 2 + part], side_in.at[part, c], part == 0)

    def each_chunk(body):
        def step(i, carry):
            body(lax.rem(i, 2) * (CHUNKS // 2) + i // 2)
            return carry

        lax.fori_loop(0, CHUNKS, step, 0)

    def run_maps():
        in_copy(0).wait()
        held["rows"] = local_maps(
            raw_ref, v_ref, beta_ref, decay_ref, keys_ref, tf_ref, x_ref, in_copy(1).wait
        )
        pl.semaphore_wait(barrier, 2 * (LINE - 1) + ROWS - 1 + 3)
        for h in (1, 0, 2, 3):
            keep = owner & (z == 2 * h + 1)

            @pl.when(jnp.logical_not(keep))
            def _():
                map_copy(h).start()

            @pl.when(keep)
            def _():
                maps_ref[z] = tf_ref[h]

    def end_maps():
        for h in range(HEADS):
            @pl.when(jnp.logical_not(owner & (z == 2 * h + 1)))
            def _():
                map_copy(h).wait_send()

    def run_reads():
        g_row, r_rows = held["rows"]
        in_copy(2).wait()
        in_copy(3).wait()
        local_reads(q_ref, keys_ref, decay_ref, x_ref, g_row, r_rows, lo_ref, lq_ref)
        gate = gate_ref[...].astype(F32)
        act_ref[...] = (gate / (1.0 + jnp.exp(-gate))) * jnp.concatenate(
            [gain_ref[...]] * HEADS, axis=1
        )

    def run_gather():
        @pl.when(owner)
        def _():
            def arrived(other):
                pltpu.make_async_remote_copy(
                    src_ref=tf_ref.at[0], dst_ref=maps_ref.at[other],
                    send_sem=map_send.at[0], recv_sem=map_recv.at[other], **at(line + other, sibling),
                ).wait_recv()

            for i in range(1, LINE):
                arrived(lax.rem(z + i, LINE))

            @pl.when(mine_core == 0)
            def _():
                arrived(z)

    def run_compose():
        @pl.when(owner)
        def _():
            m = [(maps_ref[i, 0], maps_ref[i, 1]) for i in range(LINE)]
            (p1,) = compose([m[1]], m[0])
            (q23,) = compose([m[3]], m[2])
            (q45,) = compose([m[5]], m[4])
            (q67,) = compose([m[7]], m[6])
            (p3,) = compose([q23], p1)
            (q47,) = compose([q67], q45)
            (p7,) = compose([q47], p3)
            total_ref[0] = p7[0]
            total_ref[1] = p7[1]

            @pl.when(x == 0)
            def _():
                for i, to in enumerate((3, 1, 2)):
                    line_copy(total_ref.at[1], line_ref, i, 0, to).start()

            @pl.when(x == 1)
            def _():
                for i, to in enumerate((3, 2)):
                    line_copy(total_ref, far_ref.at[0], i, 1, to).start()

            @pl.when(x == 2)
            def _():
                line_copy(total_ref, far_ref.at[1], 0, 2, 3).start()

            (p2,) = compose([m[2]], p1)
            (q46,) = compose([m[6]], q45)
            p4, p5, p6 = compose([m[4], q45, q46], p3)
            for i, (t, f) in enumerate((m[0], p1, p2, p3, p4, p5, p6)):
                pre_t_ref[i * W : (i + 1) * W] = lhs_of(t)
                pre_f_ref[i] = f

    def run_weights():
        w_copy.start()

    def run_lines():
        @pl.when(owner)
        def _():
            @pl.when(x == 0)
            def _():
                given_ref[0] = jnp.zeros((W, W), F32)

            @pl.when(x > 0)
            def _():
                line_copy(total_ref.at[1], line_ref, 0, 0, 1).wait_recv()
                given_ref[0] = line_ref[...]

            @pl.when(x > 1)
            def _():
                begin = rhs_of(line_ref[...])
                line_copy(total_ref, far_ref.at[0], 0, 1, 3).wait_recv()
                given_ref[0] = mm(lhs_of(far_ref[0, 0]), begin) + far_ref[0, 1]

            @pl.when(x == 3)
            def _():
                line_copy(total_ref, far_ref.at[1], 0, 2, 3).wait_recv()
                given_ref[0] = mm(lhs_of(far_ref[1, 0]), rhs_of(given_ref[0])) + far_ref[1, 1]

    def end_lines():
        @pl.when(owner)
        def _():
            @pl.when(x == 0)
            def _():
                for i, to in enumerate((3, 1, 2)):
                    line_copy(total_ref.at[1], line_ref, i, 0, to).wait_send()

            @pl.when(x == 1)
            def _():
                for i, to in enumerate((3, 2)):
                    line_copy(total_ref, far_ref.at[0], i, 1, to).wait_send()

            @pl.when(x == 2)
            def _():
                line_copy(total_ref, far_ref.at[1], 0, 2, 3).wait_send()

    def run_starts():
        def give(to):
            keep = (z == to) & (mine_core == 1)

            @pl.when(jnp.logical_not(keep))
            def _():
                start_copy(to, mine).start()

            @pl.when(keep)
            def _():
                start_ref[mine] = given_ref[to]

        @pl.when(owner)
        def _():
            give(0)
            for batch in ((1, 2, 3, 7), (4, 5, 6)):
                @pl.when(x == 0)
                def _():
                    for to in batch:
                        given_ref[to] = pre_f_ref[to - 1]

                @pl.when(x > 0)
                def _():
                    begin = rhs_of(given_ref[0])
                    after = [mm(pre_t_ref[(to - 1) * W : to * W], begin) for to in batch]
                    for to, part in zip(batch, after):
                        given_ref[to] = part + pre_f_ref[to - 1]

                for to in batch:
                    give(to)

        for h in range(HEADS):
            @pl.when(jnp.logical_not(owner & (z == 2 * h + 1)))
            def _():
                start_copy(0, h).wait_recv()

    def end_starts():
        @pl.when(owner)
        def _():
            for to in range(LINE):
                @pl.when(jnp.logical_not((z == to) & (mine_core == 1)))
                def _():
                    start_copy(to, mine).wait_send()

    def run_gated():
        for h in range(HEADS):
            heads_out = lo_ref[h] + mm(lq_ref[h], rhs_of(start_ref[h]))
            mean = jnp.sum(heads_out * heads_out, axis=1, keepdims=True) * (1.0 / W)
            normed = heads_out / jnp.sqrt(mean + 1e-5)
            gated_ref[:, :, h * W : (h + 1) * W] = (
                (normed * act_ref[:, h * W : (h + 1) * W]).astype(BF16).reshape(2 * RING, 16, W)
            )

    def run_project():
        w_copy.wait()
        block = [lax.rem(y + i, RING) * 2 for i in (2, 0, 1, 3)]
        rows = jnp.concatenate(
            [gated_ref[b + 1 - core] for b in block] + [gated_ref[b + core] for b in block], axis=0
        )

        def project(c):
            columns = pl.ds(pl.multiple_of(c * width, width), width)
            part = jnp.dot(rows, w_ref[:, columns], preferred_element_type=F32)
            pair_out[c] = part[:64].reshape(RING, 16, width)
            pair_copy(c, 0).start()
            pair_copy(c, 1).start()
            own_ref[c] = part[64:].reshape(RING, 16, width)

        each_chunk(project)

    def run_ring():
        def begin(c):
            pair_copy(c, 0).wait_recv()
            own_ref[c, 0] = own_ref[c, 0] + pair_in[c, 0]
            relay_copy(c).start()
            pair_copy(c, 1).wait_recv()
            own_ref[c, 1:] = own_ref[c, 1:] + pair_in[c, 1:]
            side_copy(c).start()

        def forward(c):
            relay_copy(c).wait_recv()
            block = 2 + c // (CHUNKS // 2)
            own_ref[c, block] = own_ref[c, block] + relay_in[c]
            onward_copy(c).start()

        def finish(c):
            side_copy(c).wait_recv()
            onward_copy(c).wait_recv()
            columns = pl.ds(pl.multiple_of(c * width, width), width)
            out_ref[:, columns] = (own_ref[c, 1] + side_in[0, c] + side_in[1, c]).astype(BF16)

        each_chunk(begin)
        each_chunk(forward)
        each_chunk(finish)

    def end_ring():
        def sent(c):
            pair_copy(c, 0).wait_send()
            pair_copy(c, 1).wait_send()
            relay_copy(c).wait_send()
            side_copy(c).wait_send()
            onward_copy(c).wait_send()

        each_chunk(sent)

    phases = (
        (run_maps, end_maps),
        (run_reads, None),
        (run_weights, None),
        (run_gather, None),
        (run_compose, None),
        (run_lines, end_lines),
        (run_starts, end_starts),
        (run_gated, None),
        (run_project, None),
        (run_ring, end_ring),
    )
    for run, end in phases:
        run()
    for run, end in phases:
        if end is not None:
            end()


def on_device(queries, key_vecs, values, out_gate, beta_rates, log_decay, norm_gain, w_out):
    inner, outer = w_out.shape
    width = outer // CHUNKS
    vmem = pl.BlockSpec(memory_space=pltpu.VMEM)
    hbm = pl.BlockSpec(memory_space=pl.ANY)
    dma = pltpu.SemaphoreType.DMA
    square = (W, W)
    return pl.pallas_call(
        layer_kernel,
        name="layer",
        out_shape=jax.ShapeDtypeStruct((16, outer), BF16),
        in_specs=[hbm] * 4 + [vmem] * 3 + [hbm],
        out_specs=vmem,
        scratch_shapes=[
            pltpu.VMEM((W, inner), BF16),
            pltpu.VMEM((STEPS, W, inner), BF16),
            pltpu.VMEM((STEPS, W, inner), BF16),
            pltpu.VMEM((W, inner), BF16),
            pltpu.VMEM((inner, outer), BF16),
            pltpu.VMEM((MICRO, inner), BF16),
            pltpu.VMEM((HEADS, 2) + square, F32),
            pltpu.VMEM((HEADS, MICRO, 2 * W), F32),
            pltpu.VMEM((HEADS,) + square, F32),
            pltpu.VMEM((HEADS, W, 2 * W), BF16),
            pltpu.VMEM((W, inner), F32),
            pltpu.VMEM((LINE, 2) + square, F32),
            pltpu.VMEM(((LINE - 1) * W, 2 * W), BF16),
            pltpu.VMEM((LINE - 1,) + square, F32),
            pltpu.VMEM((2,) + square, F32),
            pltpu.VMEM((2, 2) + square, F32),
            pltpu.VMEM(square, F32),
            pltpu.VMEM((LINE,) + square, F32),
            pltpu.VMEM((HEADS,) + square, F32),
            pltpu.VMEM((2 * RING, 16, inner), BF16),
            pltpu.VMEM((CHUNKS, RING, 16, width), F32),
            pltpu.VMEM((CHUNKS, RING, 16, width), F32),
            pltpu.VMEM((CHUNKS, RING, 16, width), F32),
            pltpu.VMEM((CHUNKS, 16, width), F32),
            pltpu.VMEM((2, CHUNKS, 16, width), F32),
            dma((4,)),
            dma,
            dma((HEADS,)),
            dma((LINE,)),
            dma((3,)),
            dma((3,)),
            dma((LINE,)),
            dma((HEADS,)),
            dma((2, CHUNKS)),
            dma((2, CHUNKS)),
            dma((3, CHUNKS)),
            dma((3, CHUNKS)),
        ],
        compiler_params=pltpu.CompilerParams(
            collective_id=0, has_side_effects=True, vmem_limit_bytes=56 * 1024 * 1024
        ),
    )(
        queries,
        key_vecs.transpose(1, 0, 2),
        values.transpose(1, 0, 2),
        out_gate,
        beta_rates,
        log_decay,
        norm_gain.reshape(1, W),
        w_out,
    )


def solution(mesh):
    placed = (
        P("seq", "head"),
        P("seq", None, "head"),
        P("seq", None, "head"),
        P("seq", "head"),
        P(None, "head", "seq"),
        P("head", "seq"),
        P(),
        P("head", None),
    )
    return jax.shard_map(
        on_device, mesh=mesh, in_specs=placed, out_specs=P(("seq", "head"), None), check_vma=False
    )
```

```python
import functools

import jax
import jax.numpy as jnp
from jax import lax
from jax.experimental import pallas as pl
from jax.experimental.pallas import tpu as pltpu
from jax.sharding import PartitionSpec as P

F32 = jnp.float32
BF16 = jnp.bfloat16
W = 128
STEPS = 3
MICRO = STEPS * W
HEADS = 4
GROUP = 4
BASE = 16
LINE = 8
ROWS = 4
RING = 4
CHUNKS = 4
MESH = pl.DeviceIdType.MESH


def iota(shape, dim):
    return lax.broadcasted_iota(jnp.int32, shape, dim)


def split(a):
    hi = a.astype(BF16)
    return hi, (a - hi.astype(F32)).astype(BF16)


def split3(a):
    hi, rest = a.astype(BF16), a - a.astype(BF16).astype(F32)
    return (hi,) + split(rest)


def lhs_of(a):
    return jnp.concatenate(split(a), axis=1)


def rhs_of(b):
    pair = jnp.concatenate(split(b), axis=1)
    return jnp.concatenate([pair, pair], axis=0)


def mm(left, right):
    out = jnp.dot(left, right, preferred_element_type=F32)
    half = out.shape[1] // 2
    return out[:, :half] + out[:, half:]


def mm_few(left, right):
    out = jnp.dot(left, right, preferred_element_type=F32)
    rows, columns = out.shape[0] // 2, out.shape[1] // 2
    out = out[:rows] + out[rows:]
    return out[:, :columns] + out[:, columns:]


def nt(a, b):
    return lax.dot_general(a, b, (((1,), (1,)), ((), ())), preferred_element_type=F32)


def local_maps(raw_ref, v_ref, beta_ref, decay_ref, k_ref, tf_ref, x_ref, v_wait):
    time_i, flat_i = iota((MICRO, MICRO), 0), iota((MICRO, MICRO), 1)
    to_time = (STEPS * lax.rem(flat_i, W) + flat_i // W == time_i).astype(BF16)
    raw = raw_ref[...].reshape(MICRO, HEADS * W)
    k_ref[...] = jnp.dot(to_time, raw, preferred_element_type=F32).astype(BF16)
    upto = (STEPS * iota((MICRO, W), 1) <= iota((MICRO, W), 0)).astype(BF16)
    upto = jnp.concatenate([upto] * 3, axis=1)
    decay = jnp.concatenate(split3(jnp.maximum(decay_ref[...], -110.0)), axis=1)
    g_col = nt(upto, decay)
    g_row = nt(decay, upto)
    beta = jnp.concatenate([beta_ref[j] for j in range(STEPS)], axis=1)
    b_col = nt(jnp.concatenate([to_time] * 3, axis=1), jnp.concatenate(split3(beta), axis=1))
    row_i, col_i = iota((W, W), 0), iota((W, W), 1)
    strict = row_i > col_i
    eye = (row_i == col_i).astype(F32)
    ones = jnp.ones((8, 2 * W), BF16)
    lane_block = iota((BASE, W), 1) // BASE
    r_cols, r_rows, systems, packed = [], [], [], []
    for h in range(HEADS):
        keys = k_ref[:, h * W : (h + 1) * W]
        wide = keys.astype(F32)
        squares = wide * wide
        r_c = 1.0 / jnp.sqrt(jnp.sum(squares, axis=1, keepdims=True) + 1e-6)
        r_r = 1.0 / jnp.sqrt(nt(ones, lhs_of(squares))[0:1] + 1e-6)
        r_cols.append(r_c)
        r_rows.append(r_r)
        scale = b_col[:, h : h + 1] * r_c
        blocks = {}
        for i in range(3):
            for j in range(i + 1):
                si, sj = slice(i * W, (i + 1) * W), slice(j * W, (j + 1) * W)
                gap = g_col[si, h : h + 1] - g_row[h : h + 1, sj]
                if i == j:
                    gap = jnp.where(strict, gap, 0.0)
                a = nt(keys[si], keys[sj]) * (scale[si] * r_r[:, sj]) * jnp.exp(gap)
                if i == j:
                    a = jnp.where(strict, a, 0.0)
                    packed.append(
                        sum(
                            jnp.where(lane_block == b, a[b * BASE : (b + 1) * BASE], 0.0)
                            for b in range(W // BASE)
                        )
                    )
                blocks[i, j] = a
        systems.append(blocks)
    count = len(packed)
    packed = lhs_of(jnp.concatenate(packed, axis=0))
    block_start = (col_i // BASE) * BASE
    small = [
        (iota((count, 8, W), 1) + 8 * s == iota((count, 8, W), 2) % BASE).astype(F32)
        for s in range(BASE // 8)
    ]
    for j in range(BASE - 1):
        pick = (row_i == block_start + j).astype(BF16)
        factor = jnp.dot(
            packed, jnp.concatenate([pick, pick], axis=0), preferred_element_type=F32
        ).reshape(count, BASE, W)
        first = j // 8
        row = small[first][:, j % 8 : j % 8 + 1, :]
        for s in range(first, BASE // 8):
            small[s] = small[s] - factor[:, 8 * s : 8 * s + 8, :] * row
    row_p, col_p = iota((W, 2 * W), 0), lax.rem(iota((W, 2 * W), 1), W)
    widths = [n for n in (16, 32, 64) if n >= BASE]
    same = {n: (row_p // n == col_p // n).astype(F32) for n in widths + [W]}
    low = {n: (same[2 * n] - same[n]).astype(BF16) for n in widths}
    same = {n: same[n].astype(BF16) for n in widths}
    for group in range(0, HEADS, GROUP):
        heads = range(group, group + GROUP)
        inverse = {
            (h, i): jnp.concatenate([small[s][h * 3 + i] for s in range(BASE // 8)], axis=0)
            for h in heads
            for i in range(3)
        }
        below = {n: lhs_of(systems[n[0]][n[1], n[1]]) for n in inverse}
        for width in widths:
            even = lax.rem(iota((width, W), 1) // width, 2) == 0
            left = {n: split(inv) for n, inv in inverse.items()}
            step = {}
            for n in inverse:
                rows = jnp.concatenate(left[n], axis=0)
                step[n] = mm_few(rows, below[n] * low[width])
            for n, inv in inverse.items():
                full = jnp.concatenate([jnp.concatenate(left[n], axis=1)] * (W // width), axis=0)
                rows = jnp.concatenate(split(step[n]), axis=0)
                corner = mm_few(rows, full * same[width])
                inverse[n] = jnp.concatenate(
                    [jnp.where(even, inv, 0.0), jnp.where(even, -corner, inv)], axis=0
                )
        v_wait()
        wide, right, x1, x1r, x2, x3, solved = {}, {}, {}, {}, {}, {}, {}
        values = v_ref[...].reshape(MICRO, HEADS * W)
        values = jnp.dot(to_time, values, preferred_element_type=F32)
        for h in heads:
            b_c, g_c = b_col[:, h : h + 1], g_col[:, h : h + 1]
            wide[h] = k_ref[:, h * W : (h + 1) * W].astype(F32)
            right[h] = jnp.concatenate(
                [
                    b_c * values[:, h * W : (h + 1) * W],
                    (b_c * jnp.exp(g_c) * r_cols[h]) * wide[h],
                ],
                axis=1,
            )
        for h in heads:
            x1[h] = mm(lhs_of(inverse[h, 0]), rhs_of(right[h][:W]))
        for h in heads:
            x1r[h] = rhs_of(x1[h])
            x2[h] = right[h][W : 2 * W] - mm(lhs_of(systems[h][1, 0]), x1r[h])
        for h in heads:
            x2[h] = mm(lhs_of(inverse[h, 1]), rhs_of(x2[h]))
        for h in heads:
            x3[h] = right[h][2 * W :] - mm(lhs_of(systems[h][2, 0]), x1r[h])
        for h in heads:
            x3[h] = x3[h] - mm(lhs_of(systems[h][2, 1]), rhs_of(x2[h]))
        for h in heads:
            x3[h] = mm(lhs_of(inverse[h, 2]), rhs_of(x3[h]))
        for h in heads:
            solved = jnp.concatenate([x1[h], x2[h], x3[h]], axis=0)
            x_ref[h] = solved
            g_c, g_end = g_col[:, h : h + 1], g_col[MICRO - 1 : MICRO, h : h + 1]
            tail = jnp.concatenate(split((r_cols[h] * jnp.exp(g_end - g_c)) * solved), axis=1)
            out = jnp.dot(wide[h].T.astype(BF16), tail, preferred_element_type=F32)
            out = out[:, : 2 * W] + out[:, 2 * W :]
            tf_ref[h, 0] = jnp.exp(g_end) * eye - out[:, W:]
            tf_ref[h, 1] = out[:, :W]
    return g_row, r_rows


def local_reads(q_ref, k_ref, decay_ref, x_ref, g_row, r_rows, lo_ref, lq_ref):
    decay = jnp.concatenate(split3(jnp.maximum(decay_ref[...], -110.0)), axis=1)
    upto = (iota((W, W), 1) <= iota((W, W), 0)).astype(BF16)
    q_col = nt(jnp.concatenate([upto] * 3, axis=1), decay)
    visible = iota((W, MICRO), 1) <= STEPS * iota((W, MICRO), 0) + STEPS - 1
    heads = range(HEADS)
    query = [q_ref[:, h * W : (h + 1) * W] for h in heads]
    scores = [nt(query[h], k_ref[:, h * W : (h + 1) * W]) for h in heads]
    gaps = [jnp.where(visible, q_col[:, h : h + 1] - g_row[h : h + 1, :], 0.0) for h in heads]
    scores = [jnp.where(visible, scores[h] * (r_rows[h] * jnp.exp(gaps[h])), 0.0) for h in heads]
    reads = [mm(lhs_of(scores[h]), rhs_of(x_ref[h])) for h in heads]
    for h in heads:
        lo_ref[h] = reads[h][:, :W]
        lq_ref[h] = lhs_of(jnp.exp(q_col[:, h : h + 1]) * query[h].astype(F32) - reads[h][:, W:])


def compose(lefts, right):
    out = mm(
        jnp.concatenate([lhs_of(t) for t, f in lefts], axis=0),
        rhs_of(jnp.concatenate(right, axis=1)),
    )
    return [
        (out[i * W : (i + 1) * W, :W], out[i * W : (i + 1) * W, W:] + lefts[i][1])
        for i in range(len(lefts))
    ]


def layer_kernel(
    q_hbm, k_hbm, v_hbm, gate_hbm, beta_ref, decay_ref, gain_ref, w_hbm, out_ref,
    q_ref, raw_ref, v_ref, gate_ref, w_ref, keys_ref, tf_ref, x_ref, lo_ref, lq_ref, act_ref,
    maps_ref, pre_t_ref, pre_f_ref, total_ref, far_ref, line_ref, given_ref, start_ref,
    gated_ref, pair_out, pair_in, own_ref, relay_in, side_in,
    in_sem, w_sem, map_send, map_recv, line_send, line_recv, start_send, start_recv,
    pair_send, pair_recv, ring_send, ring_recv,
):
    seq, head = lax.axis_index("seq"), lax.axis_index("head")
    x, z = seq // LINE, lax.rem(seq, LINE)
    y, core = head // 2, lax.rem(head, 2)
    line = x * LINE
    owner = core == 1
    mine, mine_core = z // 2, lax.rem(z, 2)
    width = w_ref.shape[1] // CHUNKS
    held = {}

    def at(s, h):
        return {"device_id": (s, h), "device_id_type": MESH}

    owners, served = y * 2 + 1, y * 2 + mine_core
    up = lax.rem(y + 1, RING) * 2 + core
    down = lax.rem(y + RING - 1, RING) * 2 + core
    sibling = y * 2 + 1 - core

    inputs = ((k_hbm, raw_ref), (v_hbm, v_ref), (q_hbm, q_ref), (gate_hbm, gate_ref))

    def in_copy(i):
        return pltpu.make_async_copy(*inputs[i], in_sem.at[i])

    for i in range(4):
        in_copy(i).start()
    w_copy = pltpu.make_async_copy(w_hbm, w_ref, w_sem)

    barrier = pltpu.get_barrier_semaphore()
    for i in range(1, LINE):
        pl.semaphore_signal(barrier, inc=1, **at(line + lax.rem(z + i, LINE), owners))

    @pl.when(owner)
    def _():
        for i in range(1, LINE):
            pl.semaphore_signal(barrier, inc=1, **at(line + lax.rem(z + i, LINE), sibling))
        for i in range(1, ROWS):
            pl.semaphore_signal(barrier, inc=1, **at(lax.rem(x + i, ROWS) * LINE + z, head))

    for h in (up, down, sibling):
        pl.semaphore_signal(barrier, inc=1, **at(seq, h))

    def map_copy(h):
        return pltpu.make_async_remote_copy(
            src_ref=tf_ref.at[h], dst_ref=maps_ref.at[z],
            send_sem=map_send.at[h], recv_sem=map_recv.at[z],
            **at(line + 2 * h + core, owners),
        )

    def line_copy(src, dst, send, recv, to):
        return pltpu.make_async_remote_copy(
            src_ref=src, dst_ref=dst, send_sem=line_send.at[send], recv_sem=line_recv.at[recv],
            **at(to * LINE + z, head),
        )

    def start_copy(to, h):
        return pltpu.make_async_remote_copy(
            src_ref=given_ref.at[to], dst_ref=start_ref.at[h],
            send_sem=start_send.at[to], recv_sem=start_recv.at[h], **at(line + to, served),
        )

    def pair_copy(c, kind):
        part = pl.ds(0, 1) if kind == 0 else pl.ds(1, RING - 1)
        return pltpu.make_async_remote_copy(
            src_ref=pair_out.at[c, part], dst_ref=pair_in.at[c, part],
            send_sem=pair_send.at[kind, c], recv_sem=pair_recv.at[kind, c], **at(seq, sibling),
        )

    def ring_copy(kind, c, src, dst, upward):
        return pltpu.make_async_remote_copy(
            src_ref=src, dst_ref=dst, send_sem=ring_send.at[kind, c], recv_sem=ring_recv.at[kind, c],
            **at(seq, jnp.where(upward, up, down)),
        )

    def relay_copy(c):
        return ring_copy(0, c, own_ref.at[c, 0], relay_in.at[c], c < CHUNKS // 2)

    def side_copy(c):
        part = c // (CHUNKS // 2)
        return ring_copy(1, c, own_ref.at[c, 3 - part], side_in.at[1 - part, c], part == 1)

    def onward_copy(c):
        part = c // (CHUNKS // 2)
        return ring_copy(2, c, own_ref.at[c, 2 + part], side_in.at[part, c], part == 0)

    def each_chunk(body):
        def step(i, carry):
            body(lax.rem(i, 2) * (CHUNKS // 2) + i // 2)
            return carry

        lax.fori_loop(0, CHUNKS, step, 0)

    def run_maps():
        in_copy(0).wait()
        held["rows"] = local_maps(
            raw_ref, v_ref, beta_ref, decay_ref, keys_ref, tf_ref, x_ref, in_copy(1).wait
        )
        pl.semaphore_wait(barrier, LINE - 1 + 3 + core * (LINE - 1 + ROWS - 1))
        for h in (1, 0, 2, 3):
            keep = owner & (z == 2 * h + 1)

            @pl.when(jnp.logical_not(keep))
            def _():
                map_copy(h).start()

            @pl.when(keep)
            def _():
                maps_ref[z] = tf_ref[h]

    def end_maps():
        for h in range(HEADS):
            @pl.when(jnp.logical_not(owner & (z == 2 * h + 1)))
            def _():
                map_copy(h).wait_send()

    def run_reads():
        g_row, r_rows = held["rows"]
        in_copy(2).wait()
        in_copy(3).wait()
        local_reads(q_ref, keys_ref, decay_ref, x_ref, g_row, r_rows, lo_ref, lq_ref)
        gate = gate_ref[...].astype(F32)
        act_ref[...] = (gate / (1.0 + jnp.exp(-gate))) * jnp.concatenate(
            [gain_ref[...]] * HEADS, axis=1
        )

    def run_gather():
        @pl.when(owner)
        def _():
            def arrived(other):
                pltpu.make_async_remote_copy(
                    src_ref=tf_ref.at[0], dst_ref=maps_ref.at[other],
                    send_sem=map_send.at[0], recv_sem=map_recv.at[other], **at(line + other, sibling),
                ).wait_recv()

            for i in range(1, LINE):
                arrived(lax.rem(z + i, LINE))

            @pl.when(mine_core == 0)
            def _():
                arrived(z)

    def run_compose():
        @pl.when(owner)
        def _():
            m = [(maps_ref[i, 0], maps_ref[i, 1]) for i in range(LINE)]
            (p1,) = compose([m[1]], m[0])
            (q23,) = compose([m[3]], m[2])
            (q45,) = compose([m[5]], m[4])
            (q67,) = compose([m[7]], m[6])
            (p3,) = compose([q23], p1)
            (q47,) = compose([q67], q45)
            (p7,) = compose([q47], p3)
            total_ref[0] = p7[0]
            total_ref[1] = p7[1]

            @pl.when(x == 0)
            def _():
                for i, to in enumerate((3, 1, 2)):
                    line_copy(total_ref.at[1], line_ref, i, 0, to).start()

            @pl.when(x == 1)
            def _():
                for i, to in enumerate((3, 2)):
                    line_copy(total_ref, far_ref.at[0], i, 1, to).start()

            @pl.when(x == 2)
            def _():
                line_copy(total_ref, far_ref.at[1], 0, 2, 3).start()

            (p2,) = compose([m[2]], p1)
            (q46,) = compose([m[6]], q45)
            p4, p5, p6 = compose([m[4], q45, q46], p3)
            for i, (t, f) in enumerate((m[0], p1, p2, p3, p4, p5, p6)):
                pre_t_ref[i * W : (i + 1) * W] = lhs_of(t)
                pre_f_ref[i] = f

    def run_weights():
        w_copy.start()

    def run_lines():
        @pl.when(owner)
        def _():
            @pl.when(x == 0)
            def _():
                given_ref[0] = jnp.zeros((W, W), F32)

            @pl.when(x > 0)
            def _():
                line_copy(total_ref.at[1], line_ref, 0, 0, 1).wait_recv()
                given_ref[0] = line_ref[...]

            @pl.when(x > 1)
            def _():
                begin = rhs_of(line_ref[...])
                line_copy(total_ref, far_ref.at[0], 0, 1, 3).wait_recv()
                given_ref[0] = mm(lhs_of(far_ref[0, 0]), begin) + far_ref[0, 1]

            @pl.when(x == 3)
            def _():
                line_copy(total_ref, far_ref.at[1], 0, 2, 3).wait_recv()
                given_ref[0] = mm(lhs_of(far_ref[1, 0]), rhs_of(given_ref[0])) + far_ref[1, 1]

    def end_lines():
        @pl.when(owner)
        def _():
            @pl.when(x == 0)
            def _():
                for i, to in enumerate((3, 1, 2)):
                    line_copy(total_ref.at[1], line_ref, i, 0, to).wait_send()

            @pl.when(x == 1)
            def _():
                for i, to in enumerate((3, 2)):
                    line_copy(total_ref, far_ref.at[0], i, 1, to).wait_send()

            @pl.when(x == 2)
            def _():
                line_copy(total_ref, far_ref.at[1], 0, 2, 3).wait_send()

    def run_starts():
        def give(to):
            keep = (z == to) & (mine_core == 1)

            @pl.when(jnp.logical_not(keep))
            def _():
                start_copy(to, mine).start()

            @pl.when(keep)
            def _():
                start_ref[mine] = given_ref[to]

        @pl.when(owner)
        def _():
            give(0)
            for batch in ((1, 2, 3, 7), (4, 5, 6)):
                @pl.when(x == 0)
                def _():
                    for to in batch:
                        given_ref[to] = pre_f_ref[to - 1]

                @pl.when(x > 0)
                def _():
                    begin = rhs_of(given_ref[0])
                    after = [mm(pre_t_ref[(to - 1) * W : to * W], begin) for to in batch]
                    for to, part in zip(batch, after):
                        given_ref[to] = part + pre_f_ref[to - 1]

                for to in batch:
                    give(to)

        for h in range(HEADS):
            @pl.when(jnp.logical_not(owner & (z == 2 * h + 1)))
            def _():
                start_copy(0, h).wait_recv()

    def end_starts():
        @pl.when(owner)
        def _():
            for to in range(LINE):
                @pl.when(jnp.logical_not((z == to) & (mine_core == 1)))
                def _():
                    start_copy(to, mine).wait_send()

    def run_gated():
        for h in range(HEADS):
            heads_out = lo_ref[h] + mm(lq_ref[h], rhs_of(start_ref[h]))
            mean = jnp.sum(heads_out * heads_out, axis=1, keepdims=True) * (1.0 / W)
            normed = heads_out / jnp.sqrt(mean + 1e-5)
            gated_ref[:, :, h * W : (h + 1) * W] = (
                (normed * act_ref[:, h * W : (h + 1) * W]).astype(BF16).reshape(2 * RING, 16, W)
            )

    def run_project():
        w_copy.wait()
        block = [lax.rem(y + i, RING) * 2 for i in (2, 0, 1, 3)]
        rows = jnp.concatenate(
            [gated_ref[b + 1 - core] for b in block] + [gated_ref[b + core] for b in block], axis=0
        )

        def project(c):
            columns = pl.ds(pl.multiple_of(c * width, width), width)
            part = jnp.dot(rows, w_ref[:, columns], preferred_element_type=F32)
            pair_out[c] = part[:64].reshape(RING, 16, width)
            pair_copy(c, 0).start()
            pair_copy(c, 1).start()
            own_ref[c] = part[64:].reshape(RING, 16, width)

        each_chunk(project)

    def run_ring():
        def begin(c):
            pair_copy(c, 0).wait_recv()
            own_ref[c, 0] = own_ref[c, 0] + pair_in[c, 0]
            relay_copy(c).start()
            pair_copy(c, 1).wait_recv()
            own_ref[c, 1:] = own_ref[c, 1:] + pair_in[c, 1:]
            side_copy(c).start()

        def forward(c):
            relay_copy(c).wait_recv()
            block = 2 + c // (CHUNKS // 2)
            own_ref[c, block] = own_ref[c, block] + relay_in[c]
            onward_copy(c).start()

        def finish(c):
            side_copy(c).wait_recv()
            onward_copy(c).wait_recv()
            columns = pl.ds(pl.multiple_of(c * width, width), width)
            out_ref[:, columns] = (own_ref[c, 1] + side_in[0, c] + side_in[1, c]).astype(BF16)

        each_chunk(begin)
        each_chunk(forward)
        each_chunk(finish)

    def end_ring():
        def sent(c):
            pair_copy(c, 0).wait_send()
            pair_copy(c, 1).wait_send()
            relay_copy(c).wait_send()
            side_copy(c).wait_send()
            onward_copy(c).wait_send()

        each_chunk(sent)

    phases = (
        (run_maps, end_maps),
        (run_reads, None),
        (run_weights, None),
        (run_gather, None),
        (run_compose, None),
        (run_lines, end_lines),
        (run_starts, end_starts),
        (run_gated, None),
        (run_project, None),
        (run_ring, end_ring),
    )
    for run, end in phases:
        run()
    for run, end in phases:
        if end is not None:
            end()


def on_device(queries, key_vecs, values, out_gate, beta_rates, log_decay, norm_gain, w_out):
    inner, outer = w_out.shape
    width = outer // CHUNKS
    vmem = pl.BlockSpec(memory_space=pltpu.VMEM)
    hbm = pl.BlockSpec(memory_space=pl.ANY)
    dma = pltpu.SemaphoreType.DMA
    square = (W, W)
    return pl.pallas_call(
        layer_kernel,
        name="layer",
        out_shape=jax.ShapeDtypeStruct((16, outer), BF16),
        in_specs=[hbm] * 4 + [vmem] * 3 + [hbm],
        out_specs=vmem,
        scratch_shapes=[
            pltpu.VMEM((W, inner), BF16),
            pltpu.VMEM((STEPS, W, inner), BF16),
            pltpu.VMEM((STEPS, W, inner), BF16),
            pltpu.VMEM((W, inner), BF16),
            pltpu.VMEM((inner, outer), BF16),
            pltpu.VMEM((MICRO, inner), BF16),
            pltpu.VMEM((HEADS, 2) + square, F32),
            pltpu.VMEM((HEADS, MICRO, 2 * W), F32),
            pltpu.VMEM((HEADS,) + square, F32),
            pltpu.VMEM((HEADS, W, 2 * W), BF16),
            pltpu.VMEM((W, inner), F32),
            pltpu.VMEM((LINE, 2) + square, F32),
            pltpu.VMEM(((LINE - 1) * W, 2 * W), BF16),
            pltpu.VMEM((LINE - 1,) + square, F32),
            pltpu.VMEM((2,) + square, F32),
            pltpu.VMEM((2, 2) + square, F32),
            pltpu.VMEM(square, F32),
            pltpu.VMEM((LINE,) + square, F32),
            pltpu.VMEM((HEADS,) + square, F32),
            pltpu.VMEM((2 * RING, 16, inner), BF16),
            pltpu.VMEM((CHUNKS, RING, 16, width), F32),
            pltpu.VMEM((CHUNKS, RING, 16, width), F32),
            pltpu.VMEM((CHUNKS, RING, 16, width), F32),
            pltpu.VMEM((CHUNKS, 16, width), F32),
            pltpu.VMEM((2, CHUNKS, 16, width), F32),
            dma((4,)),
            dma,
            dma((HEADS,)),
            dma((LINE,)),
            dma((3,)),
            dma((3,)),
            dma((LINE,)),
            dma((HEADS,)),
            dma((2, CHUNKS)),
            dma((2, CHUNKS)),
            dma((3, CHUNKS)),
            dma((3, CHUNKS)),
        ],
        compiler_params=pltpu.CompilerParams(
            collective_id=0, has_side_effects=True, vmem_limit_bytes=56 * 1024 * 1024
        ),
    )(
        queries,
        key_vecs.transpose(1, 0, 2),
        values.transpose(1, 0, 2),
        out_gate,
        beta_rates,
        log_decay,
        norm_gain.reshape(1, W),
        w_out,
    )


def solution(mesh):
    placed = (
        P("seq", "head"),
        P("seq", None, "head"),
        P("seq", None, "head"),
        P("seq", "head"),
        P(None, "head", "seq"),
        P("head", "seq"),
        P(),
        P("head", None),
    )
    return jax.shard_map(
        on_device, mesh=mesh, in_specs=placed, out_specs=P(("seq", "head"), None), check_vma=False
    )
```
